128 devices in a mesh: seq: 16 (over z, y_lo, core), chan: 8 (over y_hi, x).
Axes of the slice: x: 4, y: 4 (y_hi: 2, y_lo: 2; y = y_hi * 2 + y_lo), z: 4, core: 2. Of those that a mesh axis runs over, the one named last changes fastest.
Arguments:
- inputs: bfloat16 [16384, 4096], P('seq', 'chan'), may hold values from -6 to 6
- out_grad: bfloat16 [16384, 4096], P('seq', 'chan'), may hold values from -6 to 6
- out_weight: bfloat16 [4096, 4096], P('chan'), may hold values from -0.09375 to 0.09375
- filt: float32 [2048, 4096], P('seq', 'chan'), may hold values from -1.2 to 1.2
Outputs:
- grad_in: bfloat16 [16384, 4096], P('seq', 'chan')
- filt_grad: float32 [2048, 4096], P('seq', 'chan')
The draws below stay inside these ranges and needn't reach their ends.
All inputs are finite; a program needn't handle non-finite values.
Results may differ from the reference program's by a relative error of at most 0.0049.
Values may be sent and summed in bfloat16 or wider, within the bound.
A program may use at most 256 MiB of HBM per device.

```python
import math
import jax
import jax.numpy as jnp
from jax import lax

C = 4096
E = 4096
SEQ = 16384
LAGS = 2048


def draw_filt(key, part):
    key_kind, key_rate, key_fast, key_noise = jax.random.split(key, 4)
    share = 0.5
    slow_mask = jax.random.uniform(key_kind, (C,), jnp.float32) < share
    low = jnp.log(0.1 / LAGS)
    high = jnp.log(1.0 / LAGS)
    slow_rate = jnp.exp(low + (high - low) * jax.random.uniform(key_rate, (C,), jnp.float32))
    fast_rate = 1.0 / 50.0 + (1.0 / 30.0 - 1.0 / 50.0) * jax.random.uniform(key_fast, (C,), jnp.float32)
    rates = jnp.where(slow_mask, slow_rate, fast_rate)
    lag_pos = jnp.arange(LAGS, dtype=jnp.float32)[:, None]
    envelope = jnp.exp(-rates[None, :] * lag_pos)
    norming = jnp.sqrt(2.0 * rates / (1.0 - jnp.exp(-2.0 * rates * LAGS)))
    noise = jax.random.truncated_normal(key_noise, -4.0, 4.0, (LAGS, C), jnp.float32)
    return (noise * envelope * norming[None, :]).astype(jnp.float32)


def levels(rng, shape, pieces, smallest, top_value):
    gain = 1.0
    for dim, shards_of in pieces:
        heights = jax.random.uniform(jax.random.fold_in(jax.random.fold_in(rng, 6), dim), (shards_of,), jnp.float32, smallest / len(pieces), top_value / len(pieces))
        gain = gain * jnp.repeat(jnp.exp(heights), shape[dim] // shards_of).reshape((-1,) + (1,) * (len(shape) - 1 - dim))
    return gain


def centred(rng, extent, scale, limit, cuts=(), kind=jnp.bfloat16):
    drawn = jax.random.normal(rng, extent, jnp.float32) * scale
    if len(cuts) > 0:
        drawn = levels(rng, extent, cuts, -0.22, 0.18) * drawn
    return jnp.clip(drawn, min=-limit, max=limit).astype(kind)


def setup_inputs(seed: int = 0) -> dict:
    key_of = jax.random.split(jax.random.key(seed), 5)
    inputs = centred(key_of[0], (SEQ, C), 1.0, 6.0, ((0, 16), (1, 8)))
    out_grad = centred(key_of[1], (SEQ, E), 1.0, 6.0, ((0, 16), (1, 8)))
    out_weight = centred(key_of[2], (C, E), E ** -0.5, 0.09375, ((0, 8),))
    filt = draw_filt(jax.random.fold_in(key_of[4], 71), 0)
    return dict(inputs=inputs, out_grad=out_grad, out_weight=out_weight, filt=filt)


def reference(inputs, out_grad, out_weight, filt):
    grad_mix = jnp.dot(out_grad, out_weight.T, preferred_element_type=jnp.float32).astype(jnp.bfloat16)
    fft_len = SEQ + LAGS
    chan_block = math.gcd(C, 256)
    groups = C // chan_block

    def arrange(values):
        return values.astype(jnp.float32).T.reshape(groups, chan_block, values.shape[0])

    def one_group(operands):
        grads, values, filters = operands
        grad_freq = jnp.fft.rfft(grads, fft_len, axis=1)
        value_freq = jnp.fft.rfft(values, fft_len, axis=1)
        filter_freq = jnp.fft.rfft(filters, fft_len, axis=1)
        grad_part = jnp.fft.irfft(jnp.conj(filter_freq) * grad_freq, fft_len, axis=1)[:, :SEQ]
        filter_part = jnp.fft.irfft(jnp.conj(value_freq) * grad_freq, fft_len, axis=1)[:, :LAGS]
        return (grad_part, filter_part)
    grad_part, filter_part = lax.map(one_group, (arrange(grad_mix), arrange(inputs), arrange(filt)))
    grad_in = grad_part.reshape(C, SEQ).T.astype(jnp.bfloat16)
    filt_grad = filter_part.reshape(C, LAGS).T / math.sqrt(SEQ)
    return (grad_in, filt_grad)
```

```python
import math

import jax
import jax.numpy as jnp
import numpy as np
from jax import lax
from jax.experimental import pallas as pl
from jax.experimental.pallas import tpu as pltpu
from jax.sharding import PartitionSpec as P

BLOCK = 256
FRAME = 2 * BLOCK
HALF = FRAME // 2
ROWS = 8
LANES = 128


def split_table(table):
    high = table.astype(jnp.bfloat16)
    low = (table - high.astype(np.float32)).astype(jnp.bfloat16)
    return high, low


def tables(scale):
    freq = np.arange(HALF, dtype=np.int64)[:, None]
    time = np.arange(FRAME, dtype=np.int64)[None, :]
    angle = ((2 * freq + 1) * time % (2 * FRAME)).astype(np.float64) * (math.pi / FRAME)
    forward = np.concatenate([np.cos(angle), -np.sin(angle)], axis=0)
    backward = forward[:, :BLOCK].T * (2.0 / FRAME)
    result = []
    for table in (forward, backward):
        result.extend(split_table(table.astype(np.float32)))
    return result


def dot(a, b):
    return lax.dot_general(a, b, (((1,), (0,)), ((), ())), preferred_element_type=jnp.float32)


def conv_kernel(
    grad_ref, in_ref, filt_ref, fwd_hi, fwd_lo, bwd_hi, bwd_lo,
    out_ref, lag_ref, win, lag, val, acc_in, acc_lag,
):
    blocks, lags = val.shape[0], lag.shape[0]
    width = in_ref.shape[1]

    @pl.loop(0, lags)
    def _(m):
        part = filt_ref[pl.ds(pl.multiple_of(m * BLOCK, BLOCK), BLOCK), :]
        lag[m] = dot(fwd_hi[:, :BLOCK], part) + dot(fwd_lo[:, :BLOCK], part)

    @pl.loop(0, blocks)
    def _(n):
        part = in_ref[pl.ds(pl.multiple_of(n * BLOCK, BLOCK), BLOCK), :]
        val[n] = dot(fwd_hi[:, :BLOCK], part) + dot(fwd_lo[:, :BLOCK], part)

    @pl.loop(0, blocks + lags - 1)
    def _(i):
        part = grad_ref[pl.ds(pl.multiple_of(i * BLOCK, BLOCK), FRAME), :]
        win[i] = dot(fwd_hi[...], part) + dot(fwd_lo[...], part)

    @pl.loop(0, HALF // ROWS)
    def _(p):
        re = pl.ds(pl.multiple_of(p * ROWS, ROWS), ROWS)
        im = pl.ds(pl.multiple_of(HALF + p * ROWS, ROWS), ROWS)

        @pl.loop(0, width // LANES)
        def _(q):
            ch = pl.ds(pl.multiple_of(q * LANES, LANES), LANES)
            f = [(lag[m, re, ch], lag[m, im, ch]) for m in range(lags)]
            v = [(val[n, re, ch], val[n, im, ch]) for n in range(blocks)]
            a = [None] * blocks
            d = [None] * lags

            def add(total, k, w):
                r = k[0] * w[0] + k[1] * w[1]
                s = k[0] * w[1] - k[1] * w[0]
                return (r, s) if total is None else (total[0] + r, total[1] + s)

            for i in range(blocks + lags - 1):
                w = (win[i, re, ch], win[i, im, ch])
                for n in range(blocks):
                    m = i - n
                    if 0 <= m < lags:
                        a[n] = add(a[n], f[m], w)
                        d[m] = add(d[m], v[n], w)
            for n in range(blocks):
                acc_in[n, re, ch], acc_in[n, im, ch] = a[n]
            for m in range(lags):
                acc_lag[m, re, ch], acc_lag[m, im, ch] = d[m]

    @pl.loop(0, blocks)
    def _(n):
        part = acc_in[n].astype(jnp.bfloat16)
        rows = pl.ds(pl.multiple_of(n * BLOCK, BLOCK), BLOCK)
        out_ref[rows, :] = (dot(bwd_hi[...], part) + dot(bwd_lo[...], part)).astype(out_ref.dtype)

    @pl.loop(0, lags)
    def _(m):
        part = acc_lag[m].astype(jnp.bfloat16)
        rows = pl.ds(pl.multiple_of(m * BLOCK, BLOCK), BLOCK)
        lag_ref[rows, :] = (dot(bwd_hi[...], part) + dot(bwd_lo[...], part)).astype(lag_ref.dtype)


def convolve(extended, inputs, filt):
    span, width = inputs.shape
    lag_len = filt.shape[0]
    blocks, lags = span // BLOCK, lag_len // BLOCK
    vmem = pl.BlockSpec(memory_space=pltpu.VMEM)
    return pl.pallas_call(
        conv_kernel,
        out_shape=(
            jax.ShapeDtypeStruct((span, width), jnp.bfloat16),
            jax.ShapeDtypeStruct((lag_len, width), jnp.bfloat16),
        ),
        in_specs=[vmem] * 7,
        out_specs=(vmem, vmem),
        scratch_shapes=[
            pltpu.VMEM((blocks + lags - 1, FRAME, width), jnp.float32),
            pltpu.VMEM((lags, FRAME, width), jnp.float32),
            pltpu.VMEM((blocks, FRAME, width), jnp.float32),
            pltpu.VMEM((blocks, FRAME, width), jnp.float32),
            pltpu.VMEM((lags, FRAME, width), jnp.float32),
        ],
        compiler_params=pltpu.CompilerParams(vmem_limit_bytes=60 << 20),
        name="convolve",
    )(extended, inputs, filt, *tables(1.0))


def from_behind(block, axis, distance):
    devices = range(lax.axis_size(axis))
    route = [(i - distance, i) for i in devices if i - distance in devices]
    return lax.ppermute(block, axis, route)


def per_device(inputs, out_grad, out_weight, filt):
    span_len, chan_width = inputs.shape
    grad_mix = lax.dot_general(
        lax.all_gather(out_grad, "chan", axis=1, tiled=True),
        out_weight,
        (((1,), (1,)), ((), ())),
        preferred_element_type=jnp.float32,
    ).astype(jnp.bfloat16)
    whole_filter = lax.all_gather(filt.astype(jnp.bfloat16), "seq", axis=0, tiled=True)
    steps = whole_filter.shape[0] // span_len
    later = [from_behind(grad_mix, "seq", -offset) for offset in range(1, steps + 1)]
    extended = jnp.concatenate([grad_mix] + later, axis=0)
    grad_in, local_grad = convolve(extended, inputs, whole_filter)
    seq_count = lax.axis_size("seq")
    parts = lax.all_to_all(
        local_grad.reshape(seq_count, -1, chan_width), "seq", 0, 0, tiled=True
    )
    grad_scale = 1.0 / math.sqrt(span_len * seq_count)
    filt_grad = jnp.sum(parts.astype(jnp.float32), axis=0) * grad_scale
    return (grad_in, filt_grad)


def solution(mesh):
    in_specs = (P("seq", "chan"), P("seq", "chan"), P("chan", None), P("seq", "chan"))
    out_specs = (P("seq", "chan"), P("seq", "chan"))
    return jax.shard_map(
        per_device, mesh=mesh, in_specs=in_specs, out_specs=out_specs, check_vma=False
    )
```

```python
import functools
import math

import jax
import jax.numpy as jnp
import numpy as np
from jax import lax
from jax.experimental import pallas as pl
from jax.experimental.pallas import tpu as pltpu
from jax.sharding import PartitionSpec as P

MESH = pl.DeviceIdType.MESH
BLOCK = 256
FRAME = 2 * BLOCK
HALF = FRAME // 2
ROWS = 8
LANES = 128
SPANS = 16
GROUP = 4
RING = 4
SPAN = 1024
CHUNKS = SPAN // BLOCK
WIDTH = 512
LAG_LEN = 2048
LAG_ROWS = LAG_LEN // SPANS
LAGS = LAG_LEN // BLOCK
BLOCKS = GROUP * SPAN // BLOCK
WINDOWS = BLOCKS + LAGS - 1
SHARE = RING * WIDTH


def split_table(table):
    high = table.astype(jnp.bfloat16)
    low = (table - high.astype(np.float32)).astype(jnp.bfloat16)
    return high, low


def tables():
    freq = np.arange(HALF, dtype=np.int64)[:, None]
    time = np.arange(FRAME, dtype=np.int64)[None, :]
    angle = ((2 * freq + 1) * time % (2 * FRAME)).astype(np.float64) * (math.pi / FRAME)
    forward = np.concatenate([np.cos(angle), -np.sin(angle)], axis=0)
    backward = forward[:, :BLOCK].T * (2.0 / FRAME)
    result = []
    for table in (forward, backward):
        result.extend(split_table(table.astype(np.float32)))
    return result


def dot(a, b):
    return lax.dot_general(a, b, (((1,), (0,)), ((), ())), preferred_element_type=jnp.float32)


def dot_rows(a, b):
    return lax.dot_general(a, b, (((1,), (1,)), ((), ())), preferred_element_type=jnp.float32)


def at(start, size):
    return pl.ds(pl.multiple_of(start, size), size)


def kernel(
    in_ref, og_ref, w_ref, filt_ref, fwd_hi, fwd_lo, bwd_hi, bwd_lo,
    out_ref, fg_ref,
    side, other_w, filt_all, values, part, got, grad, win, lag, val, acc, acc_lag,
    lag_out, lag_got, out_buf,
    x_send, x_recv, w_send, w_recv, f_send, f_recv, v_send, v_recv,
    p_send, p_recv, h_send, h_recv, o_send, o_recv, r_send, r_recv, local_sem,
):
    s = lax.axis_index("seq")
    ch = lax.axis_index("chan")
    core = s % 2
    q = s % GROUP
    z = s // GROUP
    half = ch // RING
    x = ch % RING
    right = half * RING + (x + 1) % RING
    left = half * RING + (x + RING - 1) % RING
    mirror = (ch + RING) % (2 * RING)

    def device(seq, chan):
        return {"seq": seq, "chan": chan}

    def mate(k):
        return z * GROUP + (q + k) % GROUP

    def remote(src, dst, send, recv, seq, chan):
        return pltpu.make_async_remote_copy(
            src_ref=src, dst_ref=dst, send_sem=send, recv_sem=recv,
            device_id=device(seq, chan), device_id_type=MESH,
        )

    barrier = pltpu.get_barrier_semaphore()
    peers = [(s, right), (s, left)]
    peers += [(mate(k), mirror) for k in range(GROUP)]
    peers += [((s + k) % SPANS, ch) for k in range(1, SPANS)]
    for seq, chan in peers:
        pl.semaphore_signal(barrier, inc=1, device_id=device(seq, chan), device_id_type=MESH)
    pl.semaphore_wait(barrier, len(peers))

    def direct(t):
        rows = at(t * BLOCK, BLOCK)
        return [
            remote(og_ref.at[rows], side.at[d, rows], x_send.at[d, t], x_recv.at[d, t], s, to)
            for d, to in ((0, right), (1, left))
        ]

    def onward(t):
        first = at(t * BLOCK, BLOCK // 2)
        second = at(t * BLOCK + BLOCK // 2, BLOCK // 2)
        return [
            remote(side.at[0, first], side.at[2, first], x_send.at[2, t], x_recv.at[2, t], s, right),
            remote(side.at[1, second], side.at[2, second], x_send.at[3, t], x_recv.at[3, t], s, left),
        ]

    def weight(j):
        rows = at((core * 2 + j) * LANES, LANES)
        return remote(
            w_ref.at[rows, at((1 - half) * SHARE, SHARE)], other_w.at[rows],
            w_send.at[0, j], w_recv.at[0, j], mate(2), mirror,
        )

    def weight_mine(j):
        rows = at((core * 2 + j) * LANES, LANES)
        return remote(
            other_w.at[rows], other_w.at[rows],
            w_send.at[1, j], w_recv.at[1, j], s + 1 - 2 * core, ch,
        )

    def filter_to(k):
        to = (s + k) % SPANS
        return remote(
            filt_ref.at[:, at((to % GROUP) * LANES, LANES)], filt_all.at[at(s * LAG_ROWS, LAG_ROWS)],
            f_send.at[k], f_recv.at[k], to, ch,
        )

    def values_to(k):
        return remote(
            in_ref.at[:, at((q + k) % GROUP * LANES, LANES)], values.at[at(q * SPAN, SPAN)],
            v_send.at[k], v_recv.at[k], mate(k), ch,
        )

    def part_to(side_of, k, t):
        rows = at(t * BLOCK, BLOCK)
        return remote(
            part.at[side_of, (q + k) % GROUP, rows], got.at[side_of, q, rows],
            p_send.at[side_of, k, t], p_recv.at[side_of, k, t], mate(k), mirror if side_of else ch,
        )

    def halo(i, t):
        return remote(
            grad.at[at(i * SPAN + t * BLOCK, BLOCK)],
            grad.at[at((GROUP + i) * SPAN + t * BLOCK, BLOCK)],
            h_send.at[i, t], h_recv.at[i, t], (s + SPANS - GROUP) % SPANS, ch,
        )

    def out_to(k):
        return remote(
            out_buf.at[(q + k) % GROUP], out_ref.at[:, at(q * LANES, LANES)],
            o_send.at[k], o_recv.at[k], mate(k), ch,
        )

    def lag_to(k):
        to = (s + k) % SPANS
        return remote(
            lag_out.at[at(to * LAG_ROWS, LAG_ROWS)], lag_got.at[s],
            r_send.at[k], r_recv.at[k], to, ch,
        )

    def start(copies):
        for copy in copies:
            copy.start()

    start(direct(0))
    for j in range(2):
        weight(j).start()
    start(direct(1))
    for k in range(1, SPANS):
        filter_to(k).start()
    for k in range(1, GROUP):
        values_to(k).start()
    filter_own = pltpu.make_async_copy(
        filt_ref.at[:, at(q * LANES, LANES)], filt_all.at[at(s * LAG_ROWS, LAG_ROWS)], local_sem.at[0]
    )
    values_own = pltpu.make_async_copy(
        in_ref.at[:, at(q * LANES, LANES)], values.at[at(q * SPAN, SPAN)], local_sem.at[1]
    )
    filter_own.start()
    values_own.start()

    def pass_on(t):
        for copy in direct(t):
            copy.wait_recv()
        start(onward(t))
        if t + 2 < CHUNKS:
            start(direct(t + 2))

    def put(table, index, wide):
        table[2 * index] = wide[:, :LANES]
        table[2 * index + 1] = wide[:, LANES:]

    def transform_filter():
        filter_own.wait()
        for k in range(1, SPANS):
            filter_to(k).wait_recv()

        @pl.loop(0, LAGS // 2)
        def _(m):
            wide = jnp.concatenate(
                [filt_all[at((2 * m + e) * BLOCK, BLOCK), :] for e in range(2)], axis=1
            )
            high = wide.astype(jnp.bfloat16)
            low = (wide - high.astype(jnp.float32)).astype(jnp.bfloat16)
            put(lag, m, dot(fwd_hi[:, :BLOCK], high) + dot(fwd_lo[:, :BLOCK], high) + dot(fwd_hi[:, :BLOCK], low))

    def transform_values():
        values_own.wait()
        for k in range(1, GROUP):
            values_to(k).wait_recv()

        @pl.loop(0, BLOCKS // 2)
        def _(n):
            wide = jnp.concatenate(
                [values[at((2 * n + e) * BLOCK, BLOCK), :] for e in range(2)], axis=1
            )
            put(val, n, dot(fwd_hi[:, :BLOCK], wide) + dot(fwd_lo[:, :BLOCK], wide))

    def multiply(side_of, t):
        rows = at(t * BLOCK, BLOCK)
        total = None
        for d, block in enumerate((og_ref.at[rows], side.at[1, rows], side.at[2, rows], side.at[0, rows])):
            place = (x + d) % RING
            if side_of:
                cols = other_w[:, at(place * WIDTH, WIDTH)]
            else:
                cols = w_ref[:, at((half * RING + place) * WIDTH, WIDTH)]
            term = dot_rows(block[...], cols)
            total = term if total is None else total + term
        total = total.astype(jnp.bfloat16)
        for k in range(GROUP):
            part[side_of, k, rows] = total[:, k * LANES:(k + 1) * LANES]
        for k in range(GROUP):
            if side_of or k:
                part_to(side_of, k, t).start()

    def across(t):
        for copy in onward(t):
            copy.wait_recv()

    def add_up(t):
        rows = at(t * BLOCK, BLOCK)
        for k in range(GROUP):
            owner = (q + GROUP - k) % GROUP
            part_to(1, k, t).wait_recv()
            if k:
                part_to(0, k, t).wait_recv()
                near = got[0, owner, rows]
            else:
                near = part[0, owner, rows]
            total = near.astype(jnp.float32) + got[1, owner, rows].astype(jnp.float32)
            grad[at(owner * SPAN + t * BLOCK, BLOCK), :] = total.astype(jnp.bfloat16)
        for i in range(2):
            halo(i, t).start()

    pass_on(0)
    transform_filter()
    weight(0).wait_recv()
    weight_mine(0).start()
    pass_on(1)
    transform_values()
    across(0)
    multiply(0, 0)
    pass_on(2)
    across(1)
    multiply(0, 1)
    weight(1).wait_recv()
    weight_mine(1).start()
    for j in range(2):
        weight_mine(j).wait_recv()
    for t in range(2):
        multiply(1, t)
    pass_on(3)
    for t in range(2, CHUNKS):
        across(t)
        multiply(0, t)
        multiply(1, t)
    for t in range(CHUNKS):
        add_up(t)
    for t in range(CHUNKS):
        for i in range(2):
            halo(i, t).wait_recv()

    @pl.when(z == SPANS // GROUP - 1)
    def _():
        grad[GROUP * SPAN:, :] = jnp.zeros((2 * SPAN, LANES), jnp.bfloat16)

    @pl.loop(0, WINDOWS // 2)
    def _(i):
        wide = jnp.concatenate(
            [grad[pl.ds(pl.multiple_of((2 * i + e) * BLOCK, BLOCK), FRAME), :] for e in range(2)], axis=1
        )
        put(win, i, dot(fwd_hi[...], wide) + dot(fwd_lo[...], wide))

    last = grad[(WINDOWS - 1) * BLOCK:, :]
    win[WINDOWS - 1] = dot(fwd_hi[...], last) + dot(fwd_lo[...], last)

    def add(total, k, w):
        r = k[0] * w[0] + k[1] * w[1]
        i = k[0] * w[1] - k[1] * w[0]
        return (r, i) if total is None else (total[0] + r, total[1] + i)

    @pl.loop(0, HALF // ROWS)
    def _(p):
        re = at(p * ROWS, ROWS)
        im = at(HALF + p * ROWS, ROWS)
        f = [(lag[m, re, :], lag[m, im, :]) for m in range(LAGS)]
        sums = {}
        for i in range(WINDOWS):
            w = (win[i, re, :], win[i, im, :])
            for m in range(LAGS):
                n = i - m
                if 0 <= n < BLOCKS:
                    sums[n] = add(sums.get(n), f[m], w)
            done = i - LAGS + 1
            if done >= 0:
                acc[done, re, :], acc[done, im, :] = sums.pop(done)

    for k in (2, 3, 1, 0):
        place = (q + k) % GROUP
        for n in range(CHUNKS // 2):
            base = place * CHUNKS + 2 * n
            wide = jnp.concatenate([acc[base], acc[base + 1]], axis=1).astype(jnp.bfloat16)
            wide = (dot(bwd_hi[...], wide) + dot(bwd_lo[...], wide)).astype(jnp.bfloat16)
            for e in range(2):
                out_buf[place, (2 * n + e) * BLOCK:(2 * n + e + 1) * BLOCK, :] = wide[:, e * LANES:(e + 1) * LANES]
        if k:
            out_to(k).start()
    out_ref[:, at(q * LANES, LANES)] = out_buf[q]

    @pl.loop(0, HALF // ROWS)
    def _(p):
        re = at(p * ROWS, ROWS)
        im = at(HALF + p * ROWS, ROWS)
        sums = [None] * LAGS
        for i in range(WINDOWS):
            w = (win[i, re, :], win[i, im, :])
            for m in range(LAGS):
                n = i - m
                if 0 <= n < BLOCKS:
                    sums[m] = add(sums[m], (val[n, re, :], val[n, im, :]), w)
        for m in range(LAGS):
            acc_lag[m, re, :], acc_lag[m, im, :] = sums[m]

    for m in range(LAGS // 2):
        wide = jnp.concatenate([acc_lag[2 * m], acc_lag[2 * m + 1]], axis=1).astype(jnp.bfloat16)
        wide = (dot(bwd_hi[...], wide) + dot(bwd_lo[...], wide)).astype(jnp.bfloat16)
        for e in range(2):
            lag_out[(2 * m + e) * BLOCK:(2 * m + e + 1) * BLOCK, :] = wide[:, e * LANES:(e + 1) * LANES]
    for k in range(1, SPANS):
        lag_to(k).start()
    lag_got[s] = lag_out[at(s * LAG_ROWS, LAG_ROWS), :]

    for k in range(1, SPANS):
        lag_to(k).wait_recv()
    scale = 1.0 / math.sqrt(SPAN * SPANS)
    for c in range(GROUP):
        total = lag_got[c].astype(jnp.float32)
        for j in range(1, SPANS // GROUP):
            total = total + lag_got[j * GROUP + c].astype(jnp.float32)
        fg_ref[:, c * LANES:(c + 1) * LANES] = total * scale

    for t in range(CHUNKS):
        for copy in direct(t) + onward(t):
            copy.wait_send()
        for i in range(2):
            halo(i, t).wait_send()
        for k in range(GROUP):
            part_to(1, k, t).wait_send()
            if k:
                part_to(0, k, t).wait_send()
    for j in range(2):
        weight(j).wait_send()
        weight_mine(j).wait_send()
    for k in range(1, SPANS):
        filter_to(k).wait_send()
        lag_to(k).wait_send()
    for k in range(1, GROUP):
        values_to(k).wait_send()
        out_to(k).wait_send()
        out_to(k).wait_recv()


def per_device(inputs, out_grad, out_weight, filt):
    vmem = pl.BlockSpec(memory_space=pltpu.VMEM)
    bf16, f32 = jnp.bfloat16, jnp.float32
    pair = [(2, CHUNKS)] * 2
    counts = [(4, CHUNKS)] * 2 + [(2, 2)] * 2 + [(SPANS,)] * 2 + [(GROUP,)] * 2
    counts += [(2, GROUP, CHUNKS)] * 2 + pair + [(GROUP,)] * 2 + [(SPANS,)] * 2 + [(2,)]
    return pl.pallas_call(
        kernel,
        out_shape=(
            jax.ShapeDtypeStruct((SPAN, WIDTH), bf16),
            jax.ShapeDtypeStruct((LAG_ROWS, WIDTH), f32),
        ),
        in_specs=[vmem] * 8,
        out_specs=(vmem, vmem),
        scratch_shapes=[
            pltpu.VMEM((3, SPAN, WIDTH), bf16),
            pltpu.VMEM((WIDTH, SHARE), bf16),
            pltpu.VMEM((LAG_LEN, LANES), f32),
            pltpu.VMEM((GROUP * SPAN, LANES), bf16),
            pltpu.VMEM((2, GROUP, SPAN, LANES), bf16),
            pltpu.VMEM((2, GROUP, SPAN, LANES), bf16),
            pltpu.VMEM(((GROUP + 2) * SPAN, LANES), bf16),
            pltpu.VMEM((WINDOWS, FRAME, LANES), f32),
            pltpu.VMEM((LAGS, FRAME, LANES), f32),
            pltpu.VMEM((BLOCKS, FRAME, LANES), f32),
            pltpu.VMEM((BLOCKS, FRAME, LANES), f32),
            pltpu.VMEM((LAGS, FRAME, LANES), f32),
            pltpu.VMEM((LAG_LEN, LANES), bf16),
            pltpu.VMEM((SPANS, LAG_ROWS, LANES), bf16),
            pltpu.VMEM((GROUP, SPAN, LANES), bf16),
        ] + [pltpu.SemaphoreType.DMA(count) for count in counts],
        compiler_params=pltpu.CompilerParams(
            collective_id=0, has_side_effects=True, vmem_limit_bytes=60 << 20
        ),
        cost_estimate=pl.CostEstimate(
            flops=20_000_000_000, bytes_accessed=12 << 20, transcendentals=0
        ),
        name="hyena_back",
    )(inputs, out_grad, out_weight, filt, *tables())


def solution(mesh):
    in_specs = (P("seq", "chan"), P("seq", "chan"), P("chan", None), P("seq", "chan"))
    out_specs = (P("seq", "chan"), P("seq", "chan"))
    return jax.shard_map(
        per_device, mesh=mesh, in_specs=in_specs, out_specs=out_specs, check_vma=False
    )
```

```python
import math

import jax
import jax.numpy as jnp
import numpy as np
from jax import lax
from jax.experimental import pallas as pl
from jax.experimental.pallas import tpu as pltpu
from jax.sharding import PartitionSpec as P

MESH = pl.DeviceIdType.MESH
BLOCK = 256
FRAME = 2 * BLOCK
HALF = FRAME // 2
ROWS = 8
LANES = 128
SPANS = 16
GROUP = 4
RING = 4
SPAN = 1024
STEPS = ((0, 256), (256, 256), (512, 256), (768, 128), (896, 128))
PER_SPAN = SPAN // BLOCK
AHEAD = 2
WIDTH = 512
LAG_LEN = 2048
LAG_ROWS = LAG_LEN // SPANS
LAG_SHARE = GROUP * LAG_ROWS
LAGS = LAG_LEN // BLOCK
BLOCKS = GROUP * SPAN // BLOCK
WINDOWS = BLOCKS + LAGS - 1
SHARE = RING * WIDTH
PIECE = WIDTH // 2 // RING


def split_table(table):
    high = table.astype(jnp.bfloat16)
    low = (table - high.astype(np.float32)).astype(jnp.bfloat16)
    return high, low


def tables():
    freq = np.arange(HALF, dtype=np.int64)[:, None]
    time = np.arange(FRAME, dtype=np.int64)[None, :]
    angle = ((2 * freq + 1) * time % (2 * FRAME)).astype(np.float64) * (math.pi / FRAME)
    forward = np.concatenate([np.cos(angle), -np.sin(angle)], axis=0)
    backward = forward[:, :BLOCK].T * (2.0 / FRAME)
    result = []
    for table in (forward, backward):
        result.extend(split_table(table.astype(np.float32)))
    return result


def dot(a, b):
    return lax.dot_general(a, b, (((1,), (0,)), ((), ())), preferred_element_type=jnp.float32)


def dot_rows(a, b):
    return lax.dot_general(a, b, (((1,), (1,)), ((), ())), preferred_element_type=jnp.float32)


def at(start, size):
    return pl.ds(pl.multiple_of(start, size), size)


def kernel(
    in_ref, og_ref, w_ref, filt_ref, fwd_hi, fwd_lo, bwd_hi, bwd_lo,
    out_ref, fg_ref,
    own, own_w,
    side, other_w, filt_all, values, part, got, grad, win, lag, val, acc, acc_lag,
    lag_out, lag_got, lag_sum, out_buf,
    x_send, x_recv, w_send, w_recv, f_send, f_recv, v_send, v_recv,
    p_send, p_recv, h_send, h_recv, o_send, o_recv, r_send, r_recv, local_sem,
):
    s = lax.axis_index("seq")
    ch = lax.axis_index("chan")
    core = s % 2
    q = s % GROUP
    z = s // GROUP
    half = ch // RING
    x = ch % RING
    right = half * RING + (x + 1) % RING
    left = half * RING + (x + RING - 1) % RING
    mirror = (ch + RING) % (2 * RING)
    sibling = s + 1 - 2 * core
    sends = []

    def mate(k):
        return z * GROUP + (q + k) % GROUP

    def along(k):
        return (s + k * GROUP) % SPANS

    def remote(src, dst, send, recv, seq, chan):
        return pltpu.make_async_remote_copy(
            src_ref=src, dst_ref=dst, send_sem=send, recv_sem=recv,
            device_id={"seq": seq, "chan": chan}, device_id_type=MESH,
        )

    def start(*copies):
        for copy in copies:
            copy.start()
            sends.append(copy)

    filter_own = pltpu.make_async_copy(
        filt_ref.at[:, at(q * LANES, LANES)], filt_all.at[at(s * LAG_ROWS, LAG_ROWS)], local_sem.at[0]
    )
    own_load = pltpu.make_async_copy(og_ref, own, local_sem.at[1])
    weight_load = pltpu.make_async_copy(w_ref.at[:, at(half * SHARE, SHARE)], own_w, local_sem.at[2])
    values_own = pltpu.make_async_copy(
        in_ref.at[:, at(q * LANES, LANES)], values.at[at(q * SPAN, SPAN)], local_sem.at[3]
    )
    filter_own.start()
    own_load.start()
    weight_load.start()
    values_own.start()

    barrier = pltpu.get_barrier_semaphore()
    peers = [(s, right), (s, left)]
    peers += [(mate(k), mirror) for k in range(GROUP)]
    peers += [(mate(k), ch) for k in range(1, GROUP)]
    peers += [(along(k), ch) for k in range(1, RING)]
    for seq, chan in peers:
        pl.semaphore_signal(
            barrier, inc=1, device_id={"seq": seq, "chan": chan}, device_id_type=MESH
        )
    pl.semaphore_wait(barrier, len(peers))

    def step_rows(t):
        return pl.ds(*STEPS[t])

    def direct(t):
        rows = step_rows(t)
        return [
            remote(og_ref.at[rows], side.at[d, rows], x_send.at[d, t], x_recv.at[d, t], s, to)
            for d, to in ((0, right), (1, left))
        ]

    def onward(t):
        begin, size = STEPS[t]
        first = pl.ds(begin, size // 2)
        second = pl.ds(begin + size // 2, size // 2)
        return [
            remote(side.at[0, first], side.at[2, first], x_send.at[2, t], x_recv.at[2, t], s, right),
            remote(side.at[1, second], side.at[2, second], x_send.at[3, t], x_recv.at[3, t], s, left),
        ]

    def piece(k):
        return at(core * (WIDTH // 2) + (z + RING - k) % RING * PIECE, PIECE)

    def weight(k):
        return remote(
            w_ref.at[piece(k), at((1 - half) * SHARE, SHARE)], other_w.at[piece(k)],
            w_send.at[k], w_recv.at[k], mate(2), mirror,
        )

    def weight_along(k):
        return remote(
            other_w.at[piece(0)], other_w.at[piece(0)], w_send.at[k], w_recv.at[k], along(k), ch
        )

    def weight_over(k):
        return remote(
            other_w.at[piece(k)], other_w.at[piece(k)],
            w_send.at[RING + k], w_recv.at[RING + k], sibling, ch,
        )

    def filter_to(k):
        return remote(
            filt_ref.at[:, at((q + k) % GROUP * LANES, LANES)], filt_all.at[at(s * LAG_ROWS, LAG_ROWS)],
            f_send.at[0, k], f_recv.at[0, k], mate(k), ch,
        )

    def filter_along(k):
        rows = at(z * LAG_SHARE, LAG_SHARE)
        return remote(
            filt_all.at[rows], filt_all.at[rows], f_send.at[1, k], f_recv.at[1, k], along(k), ch
        )

    def values_to(k):
        return remote(
            in_ref.at[:, at((q + k) % GROUP * LANES, LANES)], values.at[at(q * SPAN, SPAN)],
            v_send.at[k], v_recv.at[k], mate(k), ch,
        )

    def part_to(side_of, k, t):
        rows = step_rows(t)
        return remote(
            part.at[side_of, (q + k) % GROUP, rows], got.at[side_of, q, rows],
            p_send.at[side_of, k, t], p_recv.at[side_of, k, t], mate(k), mirror if side_of else ch,
        )

    def halo(i, t):
        return remote(
            grad.at[pl.ds(i * SPAN + STEPS[t][0], STEPS[t][1])],
            grad.at[pl.ds((GROUP + i) * SPAN + STEPS[t][0], STEPS[t][1])],
            h_send.at[i, t], h_recv.at[i, t], along(RING - 1), ch,
        )

    def out_to(k):
        return remote(
            out_buf.at[(q + k) % GROUP], out_ref.at[:, at(q * LANES, LANES)],
            o_send.at[k], o_recv.at[k], mate(k), ch,
        )

    def lag_along(k):
        return remote(
            lag_out.at[at((z + k) % RING * LAG_SHARE, LAG_SHARE)], lag_got.at[z],
            r_send.at[0, k], r_recv.at[0, k], along(k), ch,
        )

    def lag_to(k):
        return remote(
            lag_sum.at[at((q + k) % GROUP * LAG_ROWS, LAG_ROWS)], fg_ref.at[:, at(q * LANES, LANES)],
            r_send.at[1, k], r_recv.at[1, k], mate(k), ch,
        )

    def pass_on(t):
        for copy in direct(t):
            copy.wait_recv()
        start(*onward(t))
        if t + AHEAD < len(STEPS):
            start(*direct(t + AHEAD))

    def put(table, first, second, wide):
        table[first] = wide[:, :LANES]
        table[second] = wide[:, LANES:]

    def forward(wide):
        width = wide.shape[0]
        return dot(fwd_hi[:, :width], wide) + dot(fwd_lo[:, :width], wide)

    def backward(wide):
        wide = wide.astype(jnp.bfloat16)
        return (dot(bwd_hi[...], wide) + dot(bwd_lo[...], wide)).astype(jnp.bfloat16)

    def transform_filter():
        for k in range(1, RING):
            filter_along(k).wait_recv()

        @pl.loop(0, LAGS // 2)
        def _(m):
            wide = jnp.concatenate(
                [filt_all[at((2 * m + e) * BLOCK, BLOCK), :] for e in range(2)], axis=1
            )
            high = wide.astype(jnp.bfloat16)
            low = (wide - high.astype(jnp.float32)).astype(jnp.bfloat16)
            put(lag, 2 * m, 2 * m + 1, forward(high) + dot(fwd_hi[:, :BLOCK], low))

    def transform_values():
        values_own.wait()
        for k in range(1, GROUP):
            values_to(k).wait_recv()

        @pl.loop(0, BLOCKS // 2)
        def _(n):
            put(val, 2 * n, 2 * n + 1, forward(jnp.concatenate(
                [values[at((2 * n + e) * BLOCK, BLOCK), :] for e in range(2)], axis=1
            )))

    def window(i):
        return grad[pl.ds(pl.multiple_of(i * BLOCK, BLOCK), FRAME), :]

    def transform_windows(first, pairs):
        @pl.loop(0, pairs)
        def _(j):
            i = first + 2 * PER_SPAN * j
            put(win, i, i + PER_SPAN, forward(jnp.concatenate([window(i), window(i + PER_SPAN)], axis=1)))

    def multiply(side_of, t):
        rows = step_rows(t)
        weights = other_w if side_of else own_w
        total = None
        for d, block in enumerate((own.at[rows], side.at[1, rows], side.at[2, rows], side.at[0, rows])):
            term = dot_rows(block[...], weights[:, at((x + d) % RING * WIDTH, WIDTH)])
            total = term if total is None else total + term
        total = total.astype(jnp.bfloat16)
        for k in range(GROUP):
            part[side_of, k, rows] = total[:, k * LANES:(k + 1) * LANES]
        for k in (2, 3, 1, 0):
            if side_of or k:
                start(part_to(side_of, k, t))

    def across(t):
        for copy in onward(t):
            copy.wait_recv()

    def add_up(t):
        rows = step_rows(t)
        for k in range(GROUP):
            owner = (q + GROUP - k) % GROUP
            part_to(1, k, t).wait_recv()
            if k:
                part_to(0, k, t).wait_recv()
                near = got[0, owner, rows]
            else:
                near = part[0, owner, rows]
            total = near.astype(jnp.float32) + got[1, owner, rows].astype(jnp.float32)
            begin, size = STEPS[t]
            grad[pl.ds(pl.multiple_of(owner * SPAN + begin, LANES), size), :] = total.astype(jnp.bfloat16)
        for i in range(2):
            start(halo(i, t))

    def edge(t):
        for i in range(2):
            halo(i, t).wait_recv()

        @pl.when(z == RING - 1)
        def _():
            for i in range(2):
                begin, size = STEPS[t]
                grad[pl.ds((GROUP + i) * SPAN + begin, size), :] = jnp.zeros((size, LANES), jnp.bfloat16)

    def add(total, k, w):
        r = k[0] * w[0] + k[1] * w[1]
        i = k[0] * w[1] - k[1] * w[0]
        return (r, i) if total is None else (total[0] + r, total[1] + i)

    def bins(p):
        return at(p * ROWS, ROWS), at(HALF + p * ROWS, ROWS)

    def sum_inputs(place, classes, fresh):
        base = place * PER_SPAN

        @pl.loop(0, HALF // ROWS)
        def _(p):
            re, im = bins(p)
            f = [(lag[m, re, :], lag[m, im, :]) for m in range(LAGS)]
            sums = [None if fresh else (acc[base + n, re, :], acc[base + n, im, :]) for n in range(PER_SPAN)]
            for i in range(PER_SPAN + LAGS - 1):
                if i % PER_SPAN in classes:
                    w = (win[base + i, re, :], win[base + i, im, :])
                    for n in range(PER_SPAN):
                        if 0 <= i - n < LAGS:
                            sums[n] = add(sums[n], f[i - n], w)
            for n in range(PER_SPAN):
                acc[base + n, re, :], acc[base + n, im, :] = sums[n]

    def sum_lags(classes, fresh):
        @pl.loop(0, HALF // ROWS)
        def _(p):
            re, im = bins(p)
            sums = [None if fresh else (acc_lag[m, re, :], acc_lag[m, im, :]) for m in range(LAGS)]
            for i in range(WINDOWS):
                if i % PER_SPAN in classes:
                    w = (win[i, re, :], win[i, im, :])
                    for m in range(LAGS):
                        n = i - m
                        if 0 <= n < BLOCKS:
                            sums[m] = add(sums[m], (val[n, re, :], val[n, im, :]), w)
            for m in range(LAGS):
                acc_lag[m, re, :], acc_lag[m, im, :] = sums[m]

    start(*direct(0))
    start(weight(0), weight(2))
    for k in range(1, GROUP):
        start(filter_to(k))
    start(*direct(1))
    for k in range(1, GROUP):
        start(values_to(k))
    weight(0).wait_recv()
    start(weight_along(1), weight_along(3), weight_over(0))
    pass_on(0)
    weight(2).wait_recv()
    start(weight_over(2))
    for k in (1, 3):
        weight_along(k).wait_recv()
        start(weight_over(k))
    filter_own.wait()
    for k in range(1, GROUP):
        filter_to(k).wait_recv()
    start(*[filter_along(k) for k in (2, 1, 3)])
    pass_on(1)
    transform_values()
    own_load.wait()
    weight_load.wait()
    across(0)
    multiply(0, 0)
    for k in range(RING):
        weight_over(k).wait_recv()
    multiply(1, 0)
    pass_on(2)
    across(1)
    multiply(1, 1)
    multiply(0, 1)
    add_up(0)
    pass_on(3)
    transform_filter()
    across(2)
    multiply(1, 2)
    multiply(0, 2)
    pass_on(4)
    add_up(1)
    edge(0)
    edge(1)
    across(3)
    multiply(1, 3)
    multiply(0, 3)
    across(4)
    multiply(1, 4)
    multiply(0, 4)
    transform_windows(0, 3)
    for k in range(GROUP):
        sum_inputs((q + k) % GROUP, (0,), True)
    sum_lags((0,), True)
    add_up(2)
    edge(2)
    transform_windows(1, 3)
    add_up(3)
    add_up(4)
    for k in range(GROUP):
        sum_inputs((q + k) % GROUP, (1,), False)
    sum_lags((1,), False)
    edge(3)
    edge(4)
    transform_windows(PER_SPAN - 2, 3)
    transform_windows(PER_SPAN - 1, 2)
    final = (WINDOWS - 1) - (WINDOWS - 1 - (PER_SPAN - 1)) % PER_SPAN
    win[final] = forward(window(final))

    def finish_span(k):
        place = (q + k) % GROUP
        sum_inputs(place, (2, 3), False)
        for n in range(PER_SPAN // 2):
            base = place * PER_SPAN + 2 * n
            wide = backward(jnp.concatenate([acc[base], acc[base + 1]], axis=1))
            for e in range(2):
                out_buf[place, (2 * n + e) * BLOCK:(2 * n + e + 1) * BLOCK, :] = wide[:, e * LANES:(e + 1) * LANES]
        if k:
            start(out_to(k))

    finish_span(2)
    finish_span(3)
    sum_lags((2, 3), False)
    for k in (2, 1, 3, 0):
        place = (z + k) % RING
        wide = backward(jnp.concatenate([acc_lag[2 * place], acc_lag[2 * place + 1]], axis=1))
        for e in range(2):
            lag_out[at((2 * place + e) * BLOCK, BLOCK), :] = wide[:, e * LANES:(e + 1) * LANES]
        if k:
            start(lag_along(k))
    finish_span(1)
    finish_span(0)
    out_ref[:, at(q * LANES, LANES)] = out_buf[q]
    total = lag_out[at(z * LAG_SHARE, LAG_SHARE), :].astype(jnp.float32)
    for k in range(1, RING):
        lag_along(k).wait_recv()
        total = total + lag_got[(z + RING - k) % RING].astype(jnp.float32)
    lag_sum[...] = total * (1.0 / math.sqrt(SPAN * SPANS))
    for k in (2, 3, 1):
        start(lag_to(k))
    fg_ref[:, at(q * LANES, LANES)] = lag_sum[at(q * LAG_ROWS, LAG_ROWS), :]
    for copy in sends:
        copy.wait_send()
    for k in range(1, GROUP):
        out_to(k).wait_recv()
        lag_to(k).wait_recv()


def hand_over(out_ref, fg_ref, out_final, fg_final):
    out_final[...] = out_ref[...]
    fg_final[...] = fg_ref[...]


def per_device(inputs, out_grad, out_weight, filt):
    vmem = pl.BlockSpec(memory_space=pltpu.VMEM)
    anywhere = pl.BlockSpec(memory_space=pl.ANY)
    bf16, f32 = jnp.bfloat16, jnp.float32
    steps = len(STEPS)
    counts = [(4, steps)] * 2 + [(2 * RING,)] * 2 + [(2, GROUP)] * 2 + [(GROUP,)] * 2
    counts += [(2, GROUP, steps)] * 2 + [(2, steps)] * 2 + [(GROUP,)] * 2 + [(2, GROUP)] * 2 + [(4,)]
    results = pl.pallas_call(
        kernel,
        out_shape=(
            jax.ShapeDtypeStruct((SPAN, WIDTH), bf16),
            jax.ShapeDtypeStruct((LAG_ROWS, WIDTH), f32),
        ),
        in_specs=[anywhere] * 4 + [vmem] * 4,
        out_specs=(vmem, vmem),
        scratch_shapes=[
            pltpu.VMEM((SPAN, WIDTH), bf16),
            pltpu.VMEM((WIDTH, SHARE), bf16),
            pltpu.VMEM((3, SPAN, WIDTH), bf16),
            pltpu.VMEM((WIDTH, SHARE), bf16),
            pltpu.VMEM((LAG_LEN, LANES), f32),
            pltpu.VMEM((GROUP * SPAN, LANES), bf16),
            pltpu.VMEM((2, GROUP, SPAN, LANES), bf16),
            pltpu.VMEM((2, GROUP, SPAN, LANES), bf16),
            pltpu.VMEM(((GROUP + 2) * SPAN, LANES), bf16),
            pltpu.VMEM((WINDOWS, FRAME, LANES), f32),
            pltpu.VMEM((LAGS, FRAME, LANES), f32),
            pltpu.VMEM((BLOCKS, FRAME, LANES), f32),
            pltpu.VMEM((BLOCKS, FRAME, LANES), f32),
            pltpu.VMEM((LAGS, FRAME, LANES), f32),
            pltpu.VMEM((LAG_LEN, LANES), bf16),
            pltpu.VMEM((RING, LAG_SHARE, LANES), bf16),
            pltpu.VMEM((LAG_SHARE, LANES), f32),
            pltpu.VMEM((GROUP, SPAN, LANES), bf16),
        ] + [pltpu.SemaphoreType.DMA(count) for count in counts],
        compiler_params=pltpu.CompilerParams(
            collective_id=0, has_side_effects=True, vmem_limit_bytes=60 << 20
        ),
        cost_estimate=pl.CostEstimate(
            flops=20_000_000_000, bytes_accessed=12 << 20, transcendentals=0
        ),
        name="hyena_back",
    )(inputs, out_grad, out_weight, filt, *tables())
    return pl.pallas_call(
        hand_over,
        out_shape=tuple(jax.ShapeDtypeStruct(r.shape, r.dtype) for r in results),
        in_specs=[vmem] * 2,
        out_specs=(vmem, vmem),
        name="hand_over",
    )(*results)


def solution(mesh):
    in_specs = (P("seq", "chan"), P("seq", "chan"), P("chan", None), P("seq", "chan"))
    out_specs = (P("seq", "chan"), P("seq", "chan"))
    return jax.shard_map(
        per_device, mesh=mesh, in_specs=in_specs, out_specs=out_specs, check_vma=False
    )
```

```python
import math

import jax
import jax.numpy as jnp
import numpy as np
from jax import lax
from jax.experimental import pallas as pl
from jax.experimental.pallas import tpu as pltpu
from jax.sharding import PartitionSpec as P

MESH = pl.DeviceIdType.MESH
BLOCK = 256
FRAME = 2 * BLOCK
HALF = FRAME // 2
ROWS = 8
LANES = 128
SPANS = 16
GROUP = 4
RING = 4
SPAN = 1024
STEPS = ((0, 256), (256, 256), (512, 256), (768, 128), (896, 128))
PER_SPAN = SPAN // BLOCK
AHEAD = 2
WIDTH = 512
LAG_LEN = 2048
LAG_ROWS = LAG_LEN // SPANS
LAG_SHARE = GROUP * LAG_ROWS
LAGS = LAG_LEN // BLOCK
BLOCKS = GROUP * SPAN // BLOCK
WINDOWS = BLOCKS + LAGS - 1
SHARE = RING * WIDTH
PIECE = WIDTH // 2 // RING


def split_table(table):
    high = table.astype(jnp.bfloat16)
    low = (table - high.astype(np.float32)).astype(jnp.bfloat16)
    return high, low


def tables():
    freq = np.concatenate([np.arange(first, HALF, 2, dtype=np.int64) for first in range(2)])[:, None]
    time = np.arange(BLOCK, dtype=np.int64)[None, :]
    angle = ((2 * freq + 1) * time % (2 * FRAME)).astype(np.float64) * (math.pi / FRAME)
    forward = np.concatenate([np.cos(angle), -np.sin(angle)], axis=0)
    backward = forward.T * (2.0 / FRAME)
    result = []
    for table in (forward, backward):
        result.extend(split_table(table.astype(np.float32)))
    return result


def dot(a, b):
    return lax.dot_general(a, b, (((1,), (0,)), ((), ())), preferred_element_type=jnp.float32)


def dot_rows(a, b):
    return lax.dot_general(a, b, (((1,), (1,)), ((), ())), preferred_element_type=jnp.float32)


def at(start, size):
    return pl.ds(pl.multiple_of(start, size), size)


def kernel(
    in_ref, og_ref, w_ref, filt_ref, fwd_hi_ref, fwd_lo_ref, bwd_hi_ref, bwd_lo_ref,
    out_ref, fg_ref,
    own, own_w, fwd_hi, fwd_lo, bwd_hi, bwd_lo, spec,
    side, other_w, filt_all, values, part, got, grad, win, lag, val, acc, acc_lag,
    lag_out, lag_got, lag_sum, out_buf,
    x_send, x_recv, w_send, w_recv, f_send, f_recv, v_send, v_recv,
    p_send, p_recv, h_send, h_recv, o_send, o_recv, r_send, r_recv, local_sem,
):
    s = lax.axis_index("seq")
    ch = lax.axis_index("chan")
    core = s % 2
    q = s % GROUP
    z = s // GROUP
    half = ch // RING
    x = ch % RING
    right = half * RING + (x + 1) % RING
    left = half * RING + (x + RING - 1) % RING
    mirror = (ch + RING) % (2 * RING)
    sibling = s + 1 - 2 * core
    sends = []

    def mate(k):
        return z * GROUP + (q + k) % GROUP

    def along(k):
        return (s + k * GROUP) % SPANS

    def remote(src, dst, send, recv, seq, chan):
        return pltpu.make_async_remote_copy(
            src_ref=src, dst_ref=dst, send_sem=send, recv_sem=recv,
            device_id={"seq": seq, "chan": chan}, device_id_type=MESH,
        )

    def start(*copies):
        for copy in copies:
            copy.start()
            sends.append(copy)

    filter_own = pltpu.make_async_copy(
        filt_ref.at[:, at(q * LANES, LANES)], filt_all.at[at(s * LAG_ROWS, LAG_ROWS)], local_sem.at[0]
    )
    own_load = pltpu.make_async_copy(og_ref, own, local_sem.at[1])
    weight_load = pltpu.make_async_copy(w_ref.at[:, at(half * SHARE, SHARE)], own_w, local_sem.at[2])
    values_own = pltpu.make_async_copy(
        in_ref.at[:, at(q * LANES, LANES)], values.at[at(q * SPAN, SPAN)], local_sem.at[3]
    )
    table_loads = [
        pltpu.make_async_copy(src, dst, local_sem.at[4 + n])
        for n, (src, dst) in enumerate((
            (fwd_hi_ref, fwd_hi), (fwd_lo_ref, fwd_lo), (bwd_hi_ref, bwd_hi), (bwd_lo_ref, bwd_lo)
        ))
    ]
    filter_own.start()
    for load in table_loads:
        load.start()
    own_load.start()
    weight_load.start()
    values_own.start()

    barrier = pltpu.get_barrier_semaphore()
    peers = [(s, right), (s, left)]
    peers += [(mate(k), mirror) for k in range(GROUP)]
    peers += [(mate(k), ch) for k in range(1, GROUP)]
    peers += [(along(k), ch) for k in range(1, RING)]
    for seq, chan in peers:
        pl.semaphore_signal(
            barrier, inc=1, device_id={"seq": seq, "chan": chan}, device_id_type=MESH
        )
    pl.semaphore_wait(barrier, len(peers))

    def step_rows(t):
        return pl.ds(*STEPS[t])

    def direct(t):
        rows = step_rows(t)
        return [
            remote(og_ref.at[rows], side.at[d, rows], x_send.at[d, t], x_recv.at[d, t], s, to)
            for d, to in ((0, right), (1, left))
        ]

    def onward(t):
        begin, size = STEPS[t]
        first = pl.ds(begin, size // 2)
        second = pl.ds(begin + size // 2, size // 2)
        return [
            remote(side.at[0, first], side.at[2, first], x_send.at[2, t], x_recv.at[2, t], s, right),
            remote(side.at[1, second], side.at[2, second], x_send.at[3, t], x_recv.at[3, t], s, left),
        ]

    def piece(k):
        return at(core * (WIDTH // 2) + (z + RING - k) % RING * PIECE, PIECE)

    def weight(k):
        return remote(
            w_ref.at[piece(k), at((1 - half) * SHARE, SHARE)], other_w.at[piece(k)],
            w_send.at[k], w_recv.at[k], mate(2), mirror,
        )

    def weight_along(k):
        return remote(
            other_w.at[piece(0)], other_w.at[piece(0)], w_send.at[k], w_recv.at[k], along(k), ch
        )

    def weight_over(k):
        return remote(
            other_w.at[piece(k)], other_w.at[piece(k)],
            w_send.at[RING + k], w_recv.at[RING + k], sibling, ch,
        )

    def filter_to(k):
        return remote(
            filt_ref.at[:, at((q + k) % GROUP * LANES, LANES)], filt_all.at[at(s * LAG_ROWS, LAG_ROWS)],
            f_send.at[0, k], f_recv.at[0, k], mate(k), ch,
        )

    def filter_along(k):
        rows = at(z * LAG_SHARE, LAG_SHARE)
        return remote(
            filt_all.at[rows], filt_all.at[rows], f_send.at[1, k], f_recv.at[1, k], along(k), ch
        )

    def values_to(k):
        return remote(
            in_ref.at[:, at((q + k) % GROUP * LANES, LANES)], values.at[at(q * SPAN, SPAN)],
            v_send.at[k], v_recv.at[k], mate(k), ch,
        )

    def part_to(side_of, k, t):
        rows = step_rows(t)
        return remote(
            part.at[side_of, (q + k) % GROUP, rows], got.at[side_of, q, rows],
            p_send.at[side_of, k, t], p_recv.at[side_of, k, t], mate(k), mirror if side_of else ch,
        )

    def halo(i, t):
        return remote(
            grad.at[pl.ds(i * SPAN + STEPS[t][0], STEPS[t][1])],
            grad.at[pl.ds((GROUP + i) * SPAN + STEPS[t][0], STEPS[t][1])],
            h_send.at[i, t], h_recv.at[i, t], along(RING - 1), ch,
        )

    def out_to(k):
        return remote(
            out_buf.at[(q + k) % GROUP], out_ref.at[:, at(q * LANES, LANES)],
            o_send.at[k], o_recv.at[k], mate(k), ch,
        )

    def lag_along(k):
        return remote(
            lag_out.at[at((z + k) % RING * LAG_SHARE, LAG_SHARE)], lag_got.at[z],
            r_send.at[0, k], r_recv.at[0, k], along(k), ch,
        )

    def lag_to(k):
        return remote(
            lag_sum.at[at((q + k) % GROUP * LAG_ROWS, LAG_ROWS)], fg_ref.at[:, at(q * LANES, LANES)],
            r_send.at[1, k], r_recv.at[1, k], mate(k), ch,
        )

    def pass_on(t):
        for copy in direct(t):
            copy.wait_recv()
        start(*onward(t))
        if t + AHEAD < len(STEPS):
            start(*direct(t + AHEAD))

    def put(table, first, second, wide):
        table[first] = wide[:, :LANES]
        table[second] = wide[:, LANES:]

    def forward(wide):
        return dot(fwd_hi[...], wide) + dot(fwd_lo[...], wide)

    def backward(wide):
        wide = wide.astype(jnp.bfloat16)
        return (dot(bwd_hi[...], wide) + dot(bwd_lo[...], wide)).astype(jnp.bfloat16)

    def transform_filter():
        for k in range(1, RING):
            filter_along(k).wait_recv()

        @pl.loop(0, LAGS // 2)
        def _(m):
            wide = jnp.concatenate(
                [filt_all[at((2 * m + e) * BLOCK, BLOCK), :] for e in range(2)], axis=1
            )
            high = wide.astype(jnp.bfloat16)
            low = (wide - high.astype(jnp.float32)).astype(jnp.bfloat16)
            put(lag, 2 * m, 2 * m + 1, forward(high) + dot(fwd_hi[...], low))

    def transform_values():
        values_own.wait()
        for k in range(1, GROUP):
            values_to(k).wait_recv()

        @pl.loop(0, BLOCKS // 2)
        def _(n):
            put(val, 2 * n, 2 * n + 1, forward(jnp.concatenate(
                [values[at((2 * n + e) * BLOCK, BLOCK), :] for e in range(2)], axis=1
            )))

    def transform_blocks(first):
        def part_at(i):
            return grad[at(i * BLOCK, BLOCK), :]

        @pl.loop(0, (WINDOWS + 1) // PER_SPAN // 2)
        def _(j):
            i = first + 2 * PER_SPAN * j
            put(spec, i, i + PER_SPAN, forward(
                jnp.concatenate([part_at(i), part_at(i + PER_SPAN)], axis=1)
            ))

    def join(first):
        @pl.loop(0, (WINDOWS - 1 - first) // PER_SPAN + 1)
        def _(j):
            i = first + PER_SPAN * j
            for n in range(4):
                rows = slice(n * HALF // 2, (n + 1) * HALF // 2)
                cross = slice((n + 2) % 4 * HALF // 2, ((n + 2) % 4 + 1) * HALF // 2)
                here, there = spec[i, rows, :], spec[i + 1, cross, :]
                win[i, rows, :] = here + there if n in (0, 3) else here - there

    def multiply(side_of, t):
        rows = step_rows(t)
        weights = other_w if side_of else own_w
        total = None
        for d, block in enumerate((own.at[rows], side.at[1, rows], side.at[2, rows], side.at[0, rows])):
            term = dot_rows(block[...], weights[:, at((x + d) % RING * WIDTH, WIDTH)])
            total = term if total is None else total + term
        total = total.astype(jnp.bfloat16)
        for k in range(GROUP):
            part[side_of, k, rows] = total[:, k * LANES:(k + 1) * LANES]
        for k in (2, 3, 1, 0):
            if side_of or k:
                start(part_to(side_of, k, t))

    def across(t):
        for copy in onward(t):
            copy.wait_recv()

    def add_up(t):
        rows = step_rows(t)
        for k in range(GROUP):
            owner = (q + GROUP - k) % GROUP
            part_to(1, k, t).wait_recv()
            if k:
                part_to(0, k, t).wait_recv()
                near = got[0, owner, rows]
            else:
                near = part[0, owner, rows]
            total = near.astype(jnp.float32) + got[1, owner, rows].astype(jnp.float32)
            begin, size = STEPS[t]
            grad[pl.ds(pl.multiple_of(owner * SPAN + begin, LANES), size), :] = total.astype(jnp.bfloat16)
        for i in range(2):
            start(halo(i, t))

    def edge(t):
        for i in range(2):
            halo(i, t).wait_recv()

        @pl.when(z == RING - 1)
        def _():
            for i in range(2):
                begin, size = STEPS[t]
                grad[pl.ds((GROUP + i) * SPAN + begin, size), :] = jnp.zeros((size, LANES), jnp.bfloat16)

    def add(total, k, w):
        r = k[0] * w[0] + k[1] * w[1]
        i = k[0] * w[1] - k[1] * w[0]
        return (r, i) if total is None else (total[0] + r, total[1] + i)

    def bins(p):
        return at(p * ROWS, ROWS), at(HALF + p * ROWS, ROWS)

    def sum_inputs(place, classes, fresh):
        base = place * PER_SPAN

        @pl.loop(0, HALF // ROWS)
        def _(p):
            re, im = bins(p)
            f = [(lag[m, re, :], lag[m, im, :]) for m in range(LAGS)]
            sums = [None if fresh else (acc[base + n, re, :], acc[base + n, im, :]) for n in range(PER_SPAN)]
            for i in range(PER_SPAN + LAGS - 1):
                if i % PER_SPAN in classes:
                    w = (win[base + i, re, :], win[base + i, im, :])
                    for n in range(PER_SPAN):
                        if 0 <= i - n < LAGS:
                            sums[n] = add(sums[n], f[i - n], w)
            for n in range(PER_SPAN):
                acc[base + n, re, :], acc[base + n, im, :] = sums[n]

    def sum_early(chosen, fresh):
        spans = [i for i in range(WINDOWS) if i % PER_SPAN == chosen]

        @pl.loop(0, HALF // ROWS)
        def _(p):
            re, im = bins(p)
            f = [(lag[m, re, :], lag[m, im, :]) for m in range(LAGS)]
            sums = {}
            for i in spans:
                w = (win[i, re, :], win[i, im, :])
                for n in range(max(0, i - LAGS + 1), min(BLOCKS - 1, i) + 1):
                    if n not in sums:
                        sums[n] = None if fresh else (acc[n, re, :], acc[n, im, :])
                    sums[n] = add(sums[n], f[i - n], w)
                    if i + PER_SPAN > n + LAGS - 1 or i + PER_SPAN >= WINDOWS:
                        acc[n, re, :], acc[n, im, :] = sums.pop(n)

    def sum_lags(classes, fresh):
        @pl.loop(0, HALF // ROWS)
        def _(p):
            re, im = bins(p)
            sums = [None if fresh else (acc_lag[m, re, :], acc_lag[m, im, :]) for m in range(LAGS)]
            for i in range(WINDOWS):
                if i % PER_SPAN in classes:
                    w = (win[i, re, :], win[i, im, :])
                    for m in range(LAGS):
                        n = i - m
                        if 0 <= n < BLOCKS:
                            sums[m] = add(sums[m], (val[n, re, :], val[n, im, :]), w)
            for m in range(LAGS):
                acc_lag[m, re, :], acc_lag[m, im, :] = sums[m]

    start(*direct(0))
    start(weight(0), weight(2))
    for k in range(1, GROUP):
        start(filter_to(k))
    start(*direct(1))
    for k in range(1, GROUP):
        start(values_to(k))
    weight(0).wait_recv()
    start(weight_along(1), weight_along(3), weight_over(0))
    pass_on(0)
    weight(2).wait_recv()
    start(weight_over(2))
    for k in (1, 3):
        weight_along(k).wait_recv()
        start(weight_over(k))
    filter_own.wait()
    for k in range(1, GROUP):
        filter_to(k).wait_recv()
    start(*[filter_along(k) for k in (2, 1, 3)])
    pass_on(1)
    for load in table_loads:
        load.wait()
    transform_values()
    own_load.wait()
    weight_load.wait()
    across(0)
    multiply(0, 0)
    for k in range(RING):
        weight_over(k).wait_recv()
    multiply(1, 0)
    pass_on(2)
    across(1)
    multiply(1, 1)
    multiply(0, 1)
    add_up(0)
    pass_on(3)
    transform_filter()
    across(2)
    multiply(1, 2)
    multiply(0, 2)
    pass_on(4)
    add_up(1)
    edge(0)
    transform_blocks(0)
    edge(1)
    transform_blocks(1)
    across(3)
    multiply(1, 3)
    multiply(0, 3)
    across(4)
    multiply(1, 4)
    multiply(0, 4)
    join(0)
    sum_early(0, True)
    sum_lags((0,), True)
    add_up(2)
    edge(2)
    transform_blocks(2)
    join(1)
    add_up(3)
    add_up(4)
    sum_early(1, False)
    sum_lags((1,), False)
    edge(3)
    edge(4)
    transform_blocks(PER_SPAN - 1)
    join(2)
    join(3)

    def finish_span(k):
        place = (q + k) % GROUP
        sum_inputs(place, (2, 3), False)
        for n in range(PER_SPAN // 2):
            base = place * PER_SPAN + 2 * n
            wide = backward(jnp.concatenate([acc[base], acc[base + 1]], axis=1))
            for e in range(2):
                out_buf[place, (2 * n + e) * BLOCK:(2 * n + e + 1) * BLOCK, :] = wide[:, e * LANES:(e + 1) * LANES]
        if k:
            start(out_to(k))

    finish_span(2)
    finish_span(3)
    sum_lags((2, 3), False)
    for k in (2, 1, 3, 0):
        place = (z + k) % RING
        wide = backward(jnp.concatenate([acc_lag[2 * place], acc_lag[2 * place + 1]], axis=1))
        for e in range(2):
            lag_out[at((2 * place + e) * BLOCK, BLOCK), :] = wide[:, e * LANES:(e + 1) * LANES]
        if k:
            start(lag_along(k))
    finish_span(1)
    finish_span(0)
    out_ref[:, at(q * LANES, LANES)] = out_buf[q]
    total = lag_out[at(z * LAG_SHARE, LAG_SHARE), :].astype(jnp.float32)
    for k in range(1, RING):
        lag_along(k).wait_recv()
        total = total + lag_got[(z + RING - k) % RING].astype(jnp.float32)
    lag_sum[...] = total * (1.0 / math.sqrt(SPAN * SPANS))
    for k in (2, 3, 1):
        start(lag_to(k))
    fg_ref[:, at(q * LANES, LANES)] = lag_sum[at(q * LAG_ROWS, LAG_ROWS), :]
    for copy in sends:
        copy.wait_send()
    for k in range(1, GROUP):
        out_to(k).wait_recv()
        lag_to(k).wait_recv()


def hand_over(out_ref, fg_ref, out_final, fg_final, out_mid, fg_mid, sems):
    parts = [(out_ref, out_mid, out_final, pl.ds(n * BLOCK, BLOCK)) for n in range(PER_SPAN)]
    parts.append((fg_ref, fg_mid, fg_final, pl.ds(0, LAG_ROWS)))
    arrive = [
        pltpu.make_async_copy(a.at[rows], b.at[rows], sems.at[0, n])
        for n, (a, b, _, rows) in enumerate(parts)
    ]
    leave = [
        pltpu.make_async_copy(b.at[rows], c.at[rows], sems.at[1, n])
        for n, (_, b, c, rows) in enumerate(parts)
    ]
    for copy in arrive:
        copy.start()
    for first, second in zip(arrive, leave):
        first.wait()
        second.start()
    for copy in leave:
        copy.wait()


def per_device(inputs, out_grad, out_weight, filt):
    vmem = pl.BlockSpec(memory_space=pltpu.VMEM)
    anywhere = pl.BlockSpec(memory_space=pl.ANY)
    bf16, f32 = jnp.bfloat16, jnp.float32
    steps = len(STEPS)
    counts = [(4, steps)] * 2 + [(2 * RING,)] * 2 + [(2, GROUP)] * 2 + [(GROUP,)] * 2
    counts += [(2, GROUP, steps)] * 2 + [(2, steps)] * 2 + [(GROUP,)] * 2 + [(2, GROUP)] * 2 + [(8,)]
    results = pl.pallas_call(
        kernel,
        out_shape=(
            jax.ShapeDtypeStruct((SPAN, WIDTH), bf16),
            jax.ShapeDtypeStruct((LAG_ROWS, WIDTH), f32),
        ),
        in_specs=[anywhere] * 8,
        out_specs=(vmem, vmem),
        scratch_shapes=[
            pltpu.VMEM((SPAN, WIDTH), bf16),
            pltpu.VMEM((WIDTH, SHARE), bf16),
            pltpu.VMEM((FRAME, BLOCK), bf16),
            pltpu.VMEM((FRAME, BLOCK), bf16),
            pltpu.VMEM((BLOCK, FRAME), bf16),
            pltpu.VMEM((BLOCK, FRAME), bf16),
            pltpu.VMEM((WINDOWS + 1, FRAME, LANES), f32),
            pltpu.VMEM((3, SPAN, WIDTH), bf16),
            pltpu.VMEM((WIDTH, SHARE), bf16),
            pltpu.VMEM((LAG_LEN, LANES), f32),
            pltpu.VMEM((GROUP * SPAN, LANES), bf16),
            pltpu.VMEM((2, GROUP, SPAN, LANES), bf16),
            pltpu.VMEM((2, GROUP, SPAN, LANES), bf16),
            pltpu.VMEM(((GROUP + 2) * SPAN, LANES), bf16),
            pltpu.VMEM((WINDOWS, FRAME, LANES), f32),
            pltpu.VMEM((LAGS, FRAME, LANES), f32),
            pltpu.VMEM((BLOCKS, FRAME, LANES), f32),
            pltpu.VMEM((BLOCKS, FRAME, LANES), f32),
            pltpu.VMEM((LAGS, FRAME, LANES), f32),
            pltpu.VMEM((LAG_LEN, LANES), bf16),
            pltpu.VMEM((RING, LAG_SHARE, LANES), bf16),
            pltpu.VMEM((LAG_SHARE, LANES), f32),
            pltpu.VMEM((GROUP, SPAN, LANES), bf16),
        ] + [pltpu.SemaphoreType.DMA(count) for count in counts],
        compiler_params=pltpu.CompilerParams(
            collective_id=0, has_side_effects=True, vmem_limit_bytes=60 << 20
        ),
        cost_estimate=pl.CostEstimate(
            flops=20_000_000_000, bytes_accessed=12 << 20, transcendentals=0
        ),
        name="hyena_back",
    )(inputs, out_grad, out_weight, filt, *tables())
    return pl.pallas_call(
        hand_over,
        out_shape=tuple(jax.ShapeDtypeStruct(r.shape, r.dtype) for r in results),
        in_specs=[anywhere] * 2,
        out_specs=(anywhere, anywhere),
        scratch_shapes=[
            pltpu.VMEM((SPAN, WIDTH), bf16),
            pltpu.VMEM((LAG_ROWS, WIDTH), f32),
            pltpu.SemaphoreType.DMA((2, PER_SPAN + 1)),
        ],
        name="hand_over",
    )(*results)


def solution(mesh):
    in_specs = (P("seq", "chan"), P("seq", "chan"), P("chan", None), P("seq", "chan"))
    out_specs = (P("seq", "chan"), P("seq", "chan"))
    return jax.shard_map(
        per_device, mesh=mesh, in_specs=in_specs, out_specs=out_specs, check_vma=False
    )
```

```python
import math

import jax
import jax.numpy as jnp
import numpy as np
from jax import lax
from jax.experimental import pallas as pl
from jax.experimental.pallas import tpu as pltpu
from jax.sharding import PartitionSpec as P

MESH = pl.DeviceIdType.MESH
BLOCK = 256
FRAME = 2 * BLOCK
HALF = FRAME // 2
ROWS = 8
LANES = 128
SPANS = 16
GROUP = 4
RING = 4
SPAN = 1024
STEPS = ((0, 256), (256, 256), (512, 256), (768, 160), (928, 96))
PER_SPAN = SPAN // BLOCK
AHEAD = 2
WIDTH = 512
LAG_LEN = 2048
LAG_ROWS = LAG_LEN // SPANS
LAG_SHARE = GROUP * LAG_ROWS
LAGS = LAG_LEN // BLOCK
BLOCKS = GROUP * SPAN // BLOCK
WINDOWS = BLOCKS + LAGS - 1
SHARE = RING * WIDTH
PIECE = WIDTH // 2 // RING


def split_table(table):
    high = table.astype(jnp.bfloat16)
    low = (table - high.astype(np.float32)).astype(jnp.bfloat16)
    return high, low


def tables():
    freq = np.concatenate([np.arange(first, HALF, 2, dtype=np.int64) for first in range(2)])[:, None]
    time = np.arange(BLOCK, dtype=np.int64)[None, :]
    angle = ((2 * freq + 1) * time % (2 * FRAME)).astype(np.float64) * (math.pi / FRAME)
    forward = np.concatenate([np.cos(angle), -np.sin(angle)], axis=0)
    backward = forward.T * (2.0 / FRAME)
    result = []
    for table in (forward, backward):
        result.extend(split_table(table.astype(np.float32)))
    return result


def dot(a, b):
    return lax.dot_general(a, b, (((1,), (0,)), ((), ())), preferred_element_type=jnp.float32)


def dot_rows(a, b):
    return lax.dot_general(a, b, (((1,), (1,)), ((), ())), preferred_element_type=jnp.float32)


def at(start, size):
    return pl.ds(pl.multiple_of(start, size), size)


def kernel(
    in_ref, og_ref, w_ref, filt_ref, fwd_hi_ref, fwd_lo_ref, bwd_hi_ref, bwd_lo_ref,
    out_ref, fg_ref,
    own, own_w, fwd_hi, fwd_lo, bwd_hi, bwd_lo, spec,
    side, other_w, filt_all, values, part, got, grad, win, lag, val, acc, acc_lag,
    lag_out, lag_got, lag_sum, out_buf,
    x_send, x_recv, w_send, w_recv, f_send, f_recv, v_send, v_recv,
    p_send, p_recv, h_send, h_recv, o_send, o_recv, r_send, r_recv, local_sem,
):
    s = lax.axis_index("seq")
    ch = lax.axis_index("chan")
    core = s % 2
    q = s % GROUP
    z = s // GROUP
    half = ch // RING
    x = ch % RING
    right = half * RING + (x + 1) % RING
    left = half * RING + (x + RING - 1) % RING
    mirror = (ch + RING) % (2 * RING)
    sibling = s + 1 - 2 * core
    sends = []

    def mate(k):
        return z * GROUP + (q + k) % GROUP

    def along(k):
        return (s + k * GROUP) % SPANS

    def remote(src, dst, send, recv, seq, chan):
        return pltpu.make_async_remote_copy(
            src_ref=src, dst_ref=dst, send_sem=send, recv_sem=recv,
            device_id={"seq": seq, "chan": chan}, device_id_type=MESH,
        )

    def start(*copies):
        for copy in copies:
            copy.start()
            sends.append(copy)

    filter_own = pltpu.make_async_copy(
        filt_ref.at[:, at(q * LANES, LANES)], filt_all.at[at(s * LAG_ROWS, LAG_ROWS)], local_sem.at[0]
    )
    own_load = pltpu.make_async_copy(og_ref, own, local_sem.at[1])
    weight_load = pltpu.make_async_copy(w_ref.at[:, at(half * SHARE, SHARE)], own_w, local_sem.at[2])
    values_own = pltpu.make_async_copy(
        in_ref.at[:, at(q * LANES, LANES)], values.at[at(q * SPAN, SPAN)], local_sem.at[3]
    )
    table_loads = [
        pltpu.make_async_copy(src, dst, local_sem.at[4 + n])
        for n, (src, dst) in enumerate((
            (fwd_hi_ref, fwd_hi), (fwd_lo_ref, fwd_lo), (bwd_hi_ref, bwd_hi), (bwd_lo_ref, bwd_lo)
        ))
    ]
    filter_own.start()
    for load in table_loads:
        load.start()
    own_load.start()
    weight_load.start()
    values_own.start()

    barrier = pltpu.get_barrier_semaphore()
    peers = [(s, right), (s, left)]
    peers += [(mate(k), mirror) for k in range(GROUP)]
    peers += [(mate(k), ch) for k in range(1, GROUP)]
    peers += [(along(k), ch) for k in range(1, RING)]
    for seq, chan in peers:
        pl.semaphore_signal(
            barrier, inc=1, device_id={"seq": seq, "chan": chan}, device_id_type=MESH
        )
    pl.semaphore_wait(barrier, len(peers))

    def step_rows(t):
        return pl.ds(*STEPS[t])

    def direct(t):
        rows = step_rows(t)
        return [
            remote(og_ref.at[rows], side.at[d, rows], x_send.at[d, t], x_recv.at[d, t], s, to)
            for d, to in ((0, right), (1, left))
        ]

    def onward(t):
        begin, size = STEPS[t]
        first = pl.ds(begin, size // 2)
        second = pl.ds(begin + size // 2, size // 2)
        return [
            remote(side.at[0, first], side.at[2, first], x_send.at[2, t], x_recv.at[2, t], s, right),
            remote(side.at[1, second], side.at[2, second], x_send.at[3, t], x_recv.at[3, t], s, left),
        ]

    def piece(k):
        return at(core * (WIDTH // 2) + (z + RING - k) % RING * PIECE, PIECE)

    def weight(k):
        return remote(
            w_ref.at[piece(k), at((1 - half) * SHARE, SHARE)], other_w.at[piece(k)],
            w_send.at[k], w_recv.at[k], mate(2), mirror,
        )

    def weight_along(k):
        return remote(
            other_w.at[piece(0)], other_w.at[piece(0)], w_send.at[k], w_recv.at[k], along(k), ch
        )

    def weight_over(k):
        return remote(
            other_w.at[piece(k)], other_w.at[piece(k)],
            w_send.at[RING + k], w_recv.at[RING + k], sibling, ch,
        )

    def filter_to(k):
        return remote(
            filt_ref.at[:, at((q + k) % GROUP * LANES, LANES)], filt_all.at[at(s * LAG_ROWS, LAG_ROWS)],
            f_send.at[0, k], f_recv.at[0, k], mate(k), ch,
        )

    def filter_along(k):
        rows = at(z * LAG_SHARE, LAG_SHARE)
        return remote(
            filt_all.at[rows], filt_all.at[rows], f_send.at[1, k], f_recv.at[1, k], along(k), ch
        )

    def values_to(k):
        return remote(
            in_ref.at[:, at((q + k) % GROUP * LANES, LANES)], values.at[at(q * SPAN, SPAN)],
            v_send.at[k], v_recv.at[k], mate(k), ch,
        )

    def part_to(side_of, k, t):
        rows = step_rows(t)
        return remote(
            part.at[side_of, (q + k) % GROUP, rows], got.at[side_of, q, rows],
            p_send.at[side_of, k, t], p_recv.at[side_of, k, t], mate(k), mirror if side_of else ch,
        )

    def halo(i, t):
        return remote(
            grad.at[pl.ds(i * SPAN + STEPS[t][0], STEPS[t][1])],
            grad.at[pl.ds((GROUP + i) * SPAN + STEPS[t][0], STEPS[t][1])],
            h_send.at[i, t], h_recv.at[i, t], along(RING - 1), ch,
        )

    def out_to(k):
        return remote(
            out_buf.at[(q + k) % GROUP], out_ref.at[:, at(q * LANES, LANES)],
            o_send.at[k], o_recv.at[k], mate(k), ch,
        )

    def lag_along(k):
        return remote(
            lag_out.at[at((z + k) % RING * LAG_SHARE, LAG_SHARE)], lag_got.at[z],
            r_send.at[0, k], r_recv.at[0, k], along(k), ch,
        )

    def lag_to(k):
        return remote(
            lag_sum.at[at((q + k) % GROUP * LAG_ROWS, LAG_ROWS)], fg_ref.at[:, at(q * LANES, LANES)],
            r_send.at[1, k], r_recv.at[1, k], mate(k), ch,
        )

    def pass_on(t):
        for copy in direct(t):
            copy.wait_recv()
        start(*onward(t))
        if t + AHEAD < len(STEPS):
            start(*direct(t + AHEAD))

    def put(table, first, second, wide):
        table[first] = wide[:, :LANES]
        table[second] = wide[:, LANES:]

    def forward(wide):
        return dot(fwd_hi[...], wide) + dot(fwd_lo[...], wide)

    def backward(wide):
        wide = wide.astype(jnp.bfloat16)
        return (dot(bwd_hi[...], wide) + dot(bwd_lo[...], wide)).astype(jnp.bfloat16)

    def transform_filter():
        for k in range(1, RING):
            filter_along(k).wait_recv()

        @pl.loop(0, LAGS // 2)
        def _(m):
            wide = jnp.concatenate(
                [filt_all[at((2 * m + e) * BLOCK, BLOCK), :] for e in range(2)], axis=1
            )
            high = wide.astype(jnp.bfloat16)
            low = (wide - high.astype(jnp.float32)).astype(jnp.bfloat16)
            put(lag, 2 * m, 2 * m + 1, forward(high) + dot(fwd_hi[...], low))

    def transform_values():
        values_own.wait()
        for k in range(1, GROUP):
            values_to(k).wait_recv()

        @pl.loop(0, BLOCKS // 2)
        def _(n):
            put(val, 2 * n, 2 * n + 1, forward(jnp.concatenate(
                [values[at((2 * n + e) * BLOCK, BLOCK), :] for e in range(2)], axis=1
            )))

    def transform_blocks(first):
        def part_at(i):
            return grad[at(i * BLOCK, BLOCK), :]

        @pl.loop(0, (WINDOWS + 1) // PER_SPAN // 2)
        def _(j):
            i = first + 2 * PER_SPAN * j
            put(spec, i, i + PER_SPAN, forward(
                jnp.concatenate([part_at(i), part_at(i + PER_SPAN)], axis=1)
            ))

    def join(first):
        @pl.loop(0, (WINDOWS - 1 - first) // PER_SPAN + 1)
        def _(j):
            i = first + PER_SPAN * j
            for n in range(4):
                rows = slice(n * HALF // 2, (n + 1) * HALF // 2)
                cross = slice((n + 2) % 4 * HALF // 2, ((n + 2) % 4 + 1) * HALF // 2)
                here, there = spec[i, rows, :], spec[i + 1, cross, :]
                win[i, rows, :] = here + there if n in (0, 3) else here - there

    def multiply(side_of, t):
        rows = step_rows(t)
        weights = other_w if side_of else own_w
        total = None
        for d, block in enumerate((own.at[rows], side.at[1, rows], side.at[2, rows], side.at[0, rows])):
            term = dot_rows(block[...], weights[:, at((x + d) % RING * WIDTH, WIDTH)])
            total = term if total is None else total + term
        total = total.astype(jnp.bfloat16)
        for k in range(GROUP):
            part[side_of, k, rows] = total[:, k * LANES:(k + 1) * LANES]
        for k in (2, 3, 1, 0):
            if side_of or k:
                start(part_to(side_of, k, t))

    def across(t):
        for copy in onward(t):
            copy.wait_recv()

    def add_up(t):
        rows = step_rows(t)
        for k in range(GROUP):
            owner = (q + GROUP - k) % GROUP
            part_to(1, k, t).wait_recv()
            if k:
                part_to(0, k, t).wait_recv()
                near = got[0, owner, rows]
            else:
                near = part[0, owner, rows]
            total = near.astype(jnp.float32) + got[1, owner, rows].astype(jnp.float32)
            begin, size = STEPS[t]
            grad[pl.ds(pl.multiple_of(owner * SPAN + begin, 2 * ROWS), size), :] = total.astype(jnp.bfloat16)
        for i in range(2):
            start(halo(i, t))

    def edge(t):
        for i in range(2):
            halo(i, t).wait_recv()

        @pl.when(z == RING - 1)
        def _():
            for i in range(2):
                begin, size = STEPS[t]
                grad[pl.ds((GROUP + i) * SPAN + begin, size), :] = jnp.zeros((size, LANES), jnp.bfloat16)

    def add(total, k, w):
        r = k[0] * w[0] + k[1] * w[1]
        i = k[0] * w[1] - k[1] * w[0]
        return (r, i) if total is None else (total[0] + r, total[1] + i)

    def bins(p):
        return at(p * ROWS, ROWS), at(HALF + p * ROWS, ROWS)

    def sum_inputs(place, classes, fresh):
        base = place * PER_SPAN

        @pl.loop(0, HALF // ROWS)
        def _(p):
            re, im = bins(p)
            f = [(lag[m, re, :], lag[m, im, :]) for m in range(LAGS)]
            sums = [None if fresh else (acc[base + n, re, :], acc[base + n, im, :]) for n in range(PER_SPAN)]
            for i in range(PER_SPAN + LAGS - 1):
                if i % PER_SPAN in classes:
                    w = (win[base + i, re, :], win[base + i, im, :])
                    for n in range(PER_SPAN):
                        if 0 <= i - n < LAGS:
                            sums[n] = add(sums[n], f[i - n], w)
            for n in range(PER_SPAN):
                acc[base + n, re, :], acc[base + n, im, :] = sums[n]

    def sum_early(chosen, fresh):
        spans = [i for i in range(WINDOWS) if i % PER_SPAN == chosen]

        @pl.loop(0, HALF // ROWS)
        def _(p):
            re, im = bins(p)
            f = [(lag[m, re, :], lag[m, im, :]) for m in range(LAGS)]
            sums = {}
            for i in spans:
                w = (win[i, re, :], win[i, im, :])
                for n in range(max(0, i - LAGS + 1), min(BLOCKS - 1, i) + 1):
                    if n not in sums:
                        sums[n] = None if fresh else (acc[n, re, :], acc[n, im, :])
                    sums[n] = add(sums[n], f[i - n], w)
                    if i + PER_SPAN > n + LAGS - 1 or i + PER_SPAN >= WINDOWS:
                        acc[n, re, :], acc[n, im, :] = sums.pop(n)

    def sum_lags(classes, fresh):
        @pl.loop(0, HALF // ROWS)
        def _(p):
            re, im = bins(p)
            sums = [None if fresh else (acc_lag[m, re, :], acc_lag[m, im, :]) for m in range(LAGS)]
            for i in range(WINDOWS):
                if i % PER_SPAN in classes:
                    w = (win[i, re, :], win[i, im, :])
                    for m in range(LAGS):
                        n = i - m
                        if 0 <= n < BLOCKS:
                            sums[m] = add(sums[m], (val[n, re, :], val[n, im, :]), w)
            for m in range(LAGS):
                acc_lag[m, re, :], acc_lag[m, im, :] = sums[m]

    start(*direct(0))
    start(weight(0), weight(2))
    for k in range(1, GROUP):
        start(filter_to(k))
    start(*direct(1))
    for k in range(1, GROUP):
        start(values_to(k))
    weight(0).wait_recv()
    start(weight_along(1), weight_along(3), weight_over(0))
    pass_on(0)
    weight(2).wait_recv()
    start(weight_over(2))
    for k in (1, 3):
        weight_along(k).wait_recv()
        start(weight_over(k))
    filter_own.wait()
    for k in range(1, GROUP):
        filter_to(k).wait_recv()
    start(*[filter_along(k) for k in (2, 1, 3)])
    pass_on(1)
    for load in table_loads:
        load.wait()
    transform_values()
    own_load.wait()
    weight_load.wait()
    across(0)
    multiply(0, 0)
    for k in range(RING):
        weight_over(k).wait_recv()
    multiply(1, 0)
    pass_on(2)
    across(1)
    multiply(1, 1)
    multiply(0, 1)
    add_up(0)
    pass_on(3)
    transform_filter()
    across(2)
    multiply(1, 2)
    multiply(0, 2)
    pass_on(4)
    add_up(1)
    edge(0)
    transform_blocks(0)
    across(3)
    multiply(1, 3)
    multiply(0, 3)
    across(4)
    multiply(1, 4)
    multiply(0, 4)
    edge(1)
    transform_blocks(1)
    join(0)
    add_up(2)
    sum_early(0, True)
    sum_lags((0,), True)
    add_up(3)
    add_up(4)
    edge(2)
    transform_blocks(2)
    join(1)
    sum_early(1, False)
    sum_lags((1,), False)
    edge(3)
    edge(4)
    transform_blocks(PER_SPAN - 1)
    join(2)
    join(3)

    def finish_span(k):
        place = (q + k) % GROUP
        sum_inputs(place, (2, 3), False)
        for n in range(PER_SPAN // 2):
            base = place * PER_SPAN + 2 * n
            wide = backward(jnp.concatenate([acc[base], acc[base + 1]], axis=1))
            for e in range(2):
                out_buf[place, (2 * n + e) * BLOCK:(2 * n + e + 1) * BLOCK, :] = wide[:, e * LANES:(e + 1) * LANES]
        if k:
            start(out_to(k))

    finish_span(2)
    sum_lags((2, 3), False)
    for k in (2, 1, 3, 0):
        place = (z + k) % RING
        wide = backward(jnp.concatenate([acc_lag[2 * place], acc_lag[2 * place + 1]], axis=1))
        for e in range(2):
            lag_out[at((2 * place + e) * BLOCK, BLOCK), :] = wide[:, e * LANES:(e + 1) * LANES]
        if k:
            start(lag_along(k))
    finish_span(3)
    finish_span(1)
    finish_span(0)
    out_ref[:, at(q * LANES, LANES)] = out_buf[q]
    total = lag_out[at(z * LAG_SHARE, LAG_SHARE), :].astype(jnp.float32)
    for k in range(1, RING):
        lag_along(k).wait_recv()
        total = total + lag_got[(z + RING - k) % RING].astype(jnp.float32)
    lag_sum[...] = total * (1.0 / math.sqrt(SPAN * SPANS))
    for k in (2, 3, 1):
        start(lag_to(k))
    fg_ref[:, at(q * LANES, LANES)] = lag_sum[at(q * LAG_ROWS, LAG_ROWS), :]
    for copy in sends:
        copy.wait_send()
    for k in range(1, GROUP):
        out_to(k).wait_recv()
        lag_to(k).wait_recv()


def hand_over(out_ref, fg_ref, out_final, fg_final, out_mid, fg_mid, sems):
    parts = [(out_ref, out_mid, out_final, pl.ds(n * BLOCK, BLOCK)) for n in range(PER_SPAN)]
    parts.append((fg_ref, fg_mid, fg_final, pl.ds(0, LAG_ROWS)))
    arrive = [
        pltpu.make_async_copy(a.at[rows], b.at[rows], sems.at[0, n])
        for n, (a, b, _, rows) in enumerate(parts)
    ]
    leave = [
        pltpu.make_async_copy(b.at[rows], c.at[rows], sems.at[1, n])
        for n, (_, b, c, rows) in enumerate(parts)
    ]
    for copy in arrive:
        copy.start()
    for first, second in zip(arrive, leave):
        first.wait()
        second.start()
    for copy in leave:
        copy.wait()


def per_device(inputs, out_grad, out_weight, filt):
    vmem = pl.BlockSpec(memory_space=pltpu.VMEM)
    anywhere = pl.BlockSpec(memory_space=pl.ANY)
    bf16, f32 = jnp.bfloat16, jnp.float32
    steps = len(STEPS)
    counts = [(4, steps)] * 2 + [(2 * RING,)] * 2 + [(2, GROUP)] * 2 + [(GROUP,)] * 2
    counts += [(2, GROUP, steps)] * 2 + [(2, steps)] * 2 + [(GROUP,)] * 2 + [(2, GROUP)] * 2 + [(8,)]
    results = pl.pallas_call(
        kernel,
        out_shape=(
            jax.ShapeDtypeStruct((SPAN, WIDTH), bf16),
            jax.ShapeDtypeStruct((LAG_ROWS, WIDTH), f32),
        ),
        in_specs=[anywhere] * 8,
        out_specs=(vmem, vmem),
        scratch_shapes=[
            pltpu.VMEM((SPAN, WIDTH), bf16),
            pltpu.VMEM((WIDTH, SHARE), bf16),
            pltpu.VMEM((FRAME, BLOCK), bf16),
            pltpu.VMEM((FRAME, BLOCK), bf16),
            pltpu.VMEM((BLOCK, FRAME), bf16),
            pltpu.VMEM((BLOCK, FRAME), bf16),
            pltpu.VMEM((WINDOWS + 1, FRAME, LANES), f32),
            pltpu.VMEM((3, SPAN, WIDTH), bf16),
            pltpu.VMEM((WIDTH, SHARE), bf16),
            pltpu.VMEM((LAG_LEN, LANES), f32),
            pltpu.VMEM((GROUP * SPAN, LANES), bf16),
            pltpu.VMEM((2, GROUP, SPAN, LANES), bf16),
            pltpu.VMEM((2, GROUP, SPAN, LANES), bf16),
            pltpu.VMEM(((GROUP + 2) * SPAN, LANES), bf16),
            pltpu.VMEM((WINDOWS, FRAME, LANES), f32),
            pltpu.VMEM((LAGS, FRAME, LANES), f32),
            pltpu.VMEM((BLOCKS, FRAME, LANES), f32),
            pltpu.VMEM((BLOCKS, FRAME, LANES), f32),
            pltpu.VMEM((LAGS, FRAME, LANES), f32),
            pltpu.VMEM((LAG_LEN, LANES), bf16),
            pltpu.VMEM((RING, LAG_SHARE, LANES), bf16),
            pltpu.VMEM((LAG_SHARE, LANES), f32),
            pltpu.VMEM((GROUP, SPAN, LANES), bf16),
        ] + [pltpu.SemaphoreType.DMA(count) for count in counts],
        compiler_params=pltpu.CompilerParams(
            collective_id=0, has_side_effects=True, vmem_limit_bytes=60 << 20
        ),
        cost_estimate=pl.CostEstimate(
            flops=20_000_000_000, bytes_accessed=12 << 20, transcendentals=0
        ),
        name="hyena_back",
    )(inputs, out_grad, out_weight, filt, *tables())
    return pl.pallas_call(
        hand_over,
        out_shape=tuple(jax.ShapeDtypeStruct(r.shape, r.dtype) for r in results),
        in_specs=[anywhere] * 2,
        out_specs=(anywhere, anywhere),
        scratch_shapes=[
            pltpu.VMEM((SPAN, WIDTH), bf16),
            pltpu.VMEM((LAG_ROWS, WIDTH), f32),
            pltpu.SemaphoreType.DMA((2, PER_SPAN + 1)),
        ],
        name="hand_over",
    )(*results)


def solution(mesh):
    in_specs = (P("seq", "chan"), P("seq", "chan"), P("chan", None), P("seq", "chan"))
    out_specs = (P("seq", "chan"), P("seq", "chan"))
    return jax.shard_map(
        per_device, mesh=mesh, in_specs=in_specs, out_specs=out_specs, check_vma=False
    )
```

```python
import math

import jax
import jax.numpy as jnp
import numpy as np
from jax import lax
from jax.experimental import pallas as pl
from jax.experimental.pallas import tpu as pltpu
from jax.sharding import PartitionSpec as P

MESH = pl.DeviceIdType.MESH
BLOCK = 256
FRAME = 2 * BLOCK
HALF = FRAME // 2
ROWS = 8
LANES = 128
SPANS = 16
GROUP = 4
RING = 4
SPAN = 1024
STEPS = ((0, 256), (256, 256), (512, 256), (768, 160), (928, 96))
PER_SPAN = SPAN // BLOCK
AHEAD = 2
WIDTH = 512
LAG_LEN = 2048
LAG_ROWS = LAG_LEN // SPANS
LAG_SHARE = GROUP * LAG_ROWS
LAGS = LAG_LEN // BLOCK
BLOCKS = GROUP * SPAN // BLOCK
WINDOWS = BLOCKS + LAGS - 1
SHARE = RING * WIDTH
PIECE = WIDTH // 2 // RING


def split_table(table):
    high = table.astype(jnp.bfloat16)
    low = (table - high.astype(np.float32)).astype(jnp.bfloat16)
    return high, low


def tables():
    freq = np.concatenate([np.arange(first, HALF, 2, dtype=np.int64) for first in range(2)])[:, None]
    time = np.arange(BLOCK, dtype=np.int64)[None, :]
    angle = ((2 * freq + 1) * time % (2 * FRAME)).astype(np.float64) * (math.pi / FRAME)
    forward = np.concatenate([np.cos(angle), -np.sin(angle)], axis=0)
    backward = forward.T * (2.0 / FRAME)
    result = []
    for table in (forward, backward):
        result.extend(split_table(table.astype(np.float32)))
    return result


def dot(a, b):
    return lax.dot_general(a, b, (((1,), (0,)), ((), ())), preferred_element_type=jnp.float32)


def dot_rows(a, b):
    return lax.dot_general(a, b, (((1,), (1,)), ((), ())), preferred_element_type=jnp.float32)


def at(start, size):
    return pl.ds(pl.multiple_of(start, size), size)


def kernel(
    in_ref, og_ref, w_ref, filt_ref, fwd_hi_ref, fwd_lo_ref, bwd_hi_ref, bwd_lo_ref,
    out_ref, fg_ref,
    own, own_w, fwd_hi, fwd_lo, bwd_hi, bwd_lo, spec,
    side, other_w, filt_all, values, part, got, grad, win, lag, val, acc, acc_lag,
    lag_out, lag_got, lag_sum, out_buf,
    x_send, x_recv, w_send, w_recv, f_send, f_recv, v_send, v_recv,
    p_send, p_recv, h_send, h_recv, o_send, o_recv, r_send, r_recv, local_sem,
):
    s = lax.axis_index("seq")
    ch = lax.axis_index("chan")
    core = s % 2
    q = s % GROUP
    z = s // GROUP
    half = ch // RING
    x = ch % RING
    right = half * RING + (x + 1) % RING
    left = half * RING + (x + RING - 1) % RING
    mirror = (ch + RING) % (2 * RING)
    sibling = s + 1 - 2 * core
    sends = []

    def mate(k):
        return z * GROUP + (q + k) % GROUP

    def along(k):
        return (s + k * GROUP) % SPANS

    def remote(src, dst, send, recv, seq, chan):
        return pltpu.make_async_remote_copy(
            src_ref=src, dst_ref=dst, send_sem=send, recv_sem=recv,
            device_id={"seq": seq, "chan": chan}, device_id_type=MESH,
        )

    def start(*copies):
        for copy in copies:
            copy.start()
            sends.append(copy)

    filter_own = pltpu.make_async_copy(
        filt_ref.at[:, at(q * LANES, LANES)], filt_all.at[at(s * LAG_ROWS, LAG_ROWS)], local_sem.at[0]
    )
    own_load = pltpu.make_async_copy(og_ref, own, local_sem.at[1])
    weight_load = pltpu.make_async_copy(w_ref.at[:, at(half * SHARE, SHARE)], own_w, local_sem.at[2])
    values_own = pltpu.make_async_copy(
        in_ref.at[:, at(q * LANES, LANES)], values.at[at(q * SPAN, SPAN)], local_sem.at[3]
    )
    table_loads = [
        pltpu.make_async_copy(src, dst, local_sem.at[4 + n])
        for n, (src, dst) in enumerate((
            (fwd_hi_ref, fwd_hi), (fwd_lo_ref, fwd_lo), (bwd_hi_ref, bwd_hi), (bwd_lo_ref, bwd_lo)
        ))
    ]
    filter_own.start()
    for load in table_loads:
        load.start()
    own_load.start()
    weight_load.start()
    values_own.start()

    barrier = pltpu.get_barrier_semaphore()
    peers = [(s, right), (s, left)]
    peers += [(mate(k), mirror) for k in range(GROUP)]
    peers += [(mate(k), ch) for k in range(1, GROUP)]
    peers += [(along(k), ch) for k in range(1, RING)]
    for seq, chan in peers:
        pl.semaphore_signal(
            barrier, inc=1, device_id={"seq": seq, "chan": chan}, device_id_type=MESH
        )
    pl.semaphore_wait(barrier, len(peers))

    def step_rows(t):
        return pl.ds(*STEPS[t])

    def direct(t):
        rows = step_rows(t)
        return [
            remote(og_ref.at[rows], side.at[d, rows], x_send.at[d, t], x_recv.at[d, t], s, to)
            for d, to in ((0, right), (1, left))
        ]

    def onward(t):
        begin, size = STEPS[t]
        first = pl.ds(begin, size // 2)
        second = pl.ds(begin + size // 2, size // 2)
        return [
            remote(side.at[0, first], side.at[2, first], x_send.at[2, t], x_recv.at[2, t], s, right),
            remote(side.at[1, second], side.at[2, second], x_send.at[3, t], x_recv.at[3, t], s, left),
        ]

    def piece(k):
        return at(core * (WIDTH // 2) + (z + RING - k) % RING * PIECE, PIECE)

    def weight(k):
        return remote(
            w_ref.at[piece(k), at((1 - half) * SHARE, SHARE)], other_w.at[piece(k)],
            w_send.at[k], w_recv.at[k], mate(2), mirror,
        )

    def weight_along(k):
        return remote(
            other_w.at[piece(0)], other_w.at[piece(0)], w_send.at[k], w_recv.at[k], along(k), ch
        )

    def weight_over(k):
        return remote(
            other_w.at[piece(k)], other_w.at[piece(k)],
            w_send.at[RING + k], w_recv.at[RING + k], sibling, ch,
        )

    def filter_to(k):
        return remote(
            filt_ref.at[:, at((q + k) % GROUP * LANES, LANES)], filt_all.at[at(s * LAG_ROWS, LAG_ROWS)],
            f_send.at[0, k], f_recv.at[0, k], mate(k), ch,
        )

    def filter_along(k):
        rows = at(z * LAG_SHARE, LAG_SHARE)
        return remote(
            filt_all.at[rows], filt_all.at[rows], f_send.at[1, k], f_recv.at[1, k], along(k), ch
        )

    def values_to(k):
        return remote(
            in_ref.at[:, at((q + k) % GROUP * LANES, LANES)], values.at[at(q * SPAN, SPAN)],
            v_send.at[k], v_recv.at[k], mate(k), ch,
        )

    def part_to(side_of, k, t):
        rows = step_rows(t)
        return remote(
            part.at[side_of, (q + k) % GROUP, rows], got.at[side_of, q, rows],
            p_send.at[side_of, k, t], p_recv.at[side_of, k, t], mate(k), mirror if side_of else ch,
        )

    def halo(i, t):
        return remote(
            grad.at[pl.ds(i * SPAN + STEPS[t][0], STEPS[t][1])],
            grad.at[pl.ds((GROUP + i) * SPAN + STEPS[t][0], STEPS[t][1])],
            h_send.at[i, t], h_recv.at[i, t], along(RING - 1), ch,
        )

    def out_to(k):
        return remote(
            out_buf.at[(q + k) % GROUP], out_ref.at[:, at(q * LANES, LANES)],
            o_send.at[k], o_recv.at[k], mate(k), ch,
        )

    def lag_along(k):
        return remote(
            lag_out.at[at((z + k) % RING * LAG_SHARE, LAG_SHARE)], lag_got.at[z],
            r_send.at[0, k], r_recv.at[0, k], along(k), ch,
        )

    def lag_to(k):
        return remote(
            lag_sum.at[at((q + k) % GROUP * LAG_ROWS, LAG_ROWS)], fg_ref.at[:, at(q * LANES, LANES)],
            r_send.at[1, k], r_recv.at[1, k], mate(k), ch,
        )

    def pass_on(t):
        for copy in direct(t):
            copy.wait_recv()
        start(*onward(t))
        if t + AHEAD < len(STEPS):
            start(*direct(t + AHEAD))

    def put(table, first, second, wide):
        table[first] = wide[:, :LANES]
        table[second] = wide[:, LANES:]

    def forward(wide):
        return dot(fwd_hi[...], wide) + dot(fwd_lo[...], wide)

    def backward(wide):
        wide = wide.astype(jnp.bfloat16)
        return (dot(bwd_hi[...], wide) + dot(bwd_lo[...], wide)).astype(jnp.bfloat16)

    def transform_filter():
        for k in range(1, RING):
            filter_along(k).wait_recv()

        @pl.loop(0, LAGS // 2)
        def _(m):
            wide = jnp.concatenate(
                [filt_all[at((2 * m + e) * BLOCK, BLOCK), :] for e in range(2)], axis=1
            )
            high = wide.astype(jnp.bfloat16)
            low = (wide - high.astype(jnp.float32)).astype(jnp.bfloat16)
            put(lag, 2 * m, 2 * m + 1, forward(high) + dot(fwd_hi[...], low))

    def transform_values():
        values_own.wait()
        for k in range(1, GROUP):
            values_to(k).wait_recv()

        @pl.loop(0, BLOCKS // 2)
        def _(n):
            put(val, 2 * n, 2 * n + 1, forward(jnp.concatenate(
                [values[at((2 * n + e) * BLOCK, BLOCK), :] for e in range(2)], axis=1
            )))

    def transform_blocks(first):
        def part_at(i):
            return grad[at(i * BLOCK, BLOCK), :]

        @pl.loop(0, (WINDOWS + 1) // PER_SPAN // 2)
        def _(j):
            i = first + 2 * PER_SPAN * j
            put(spec, i, i + PER_SPAN, forward(
                jnp.concatenate([part_at(i), part_at(i + PER_SPAN)], axis=1)
            ))

    def join(first):
        @pl.loop(0, (WINDOWS - 1 - first) // PER_SPAN + 1)
        def _(j):
            i = first + PER_SPAN * j
            for n in range(4):
                rows = slice(n * HALF // 2, (n + 1) * HALF // 2)
                cross = slice((n + 2) % 4 * HALF // 2, ((n + 2) % 4 + 1) * HALF // 2)
                here, there = spec[i, rows, :], spec[i + 1, cross, :]
                win[i, rows, :] = here + there if n in (0, 3) else here - there

    def multiply(side_of, t):
        rows = step_rows(t)
        weights = other_w if side_of else own_w
        total = None
        for d, block in enumerate((own.at[rows], side.at[1, rows], side.at[2, rows], side.at[0, rows])):
            term = dot_rows(block[...], weights[:, at((x + d) % RING * WIDTH, WIDTH)])
            total = term if total is None else total + term
        total = total.astype(jnp.bfloat16)
        for k in range(GROUP):
            part[side_of, k, rows] = total[:, k * LANES:(k + 1) * LANES]
        for k in (2, 3, 1, 0):
            if side_of or k:
                start(part_to(side_of, k, t))

    def across(t):
        for copy in onward(t):
            copy.wait_recv()

    def add_up(t):
        rows = step_rows(t)
        for k in range(GROUP):
            owner = (q + GROUP - k) % GROUP
            part_to(1, k, t).wait_recv()
            if k:
                part_to(0, k, t).wait_recv()
                near = got[0, owner, rows]
            else:
                near = part[0, owner, rows]
            total = near.astype(jnp.float32) + got[1, owner, rows].astype(jnp.float32)
            begin, size = STEPS[t]
            grad[pl.ds(pl.multiple_of(owner * SPAN + begin, 2 * ROWS), size), :] = total.astype(jnp.bfloat16)
        for i in range(2):
            start(halo(i, t))

    def edge(t):
        for i in range(2):
            halo(i, t).wait_recv()

        @pl.when(z == RING - 1)
        def _():
            for i in range(2):
                begin, size = STEPS[t]
                grad[pl.ds((GROUP + i) * SPAN + begin, size), :] = jnp.zeros((size, LANES), jnp.bfloat16)

    def triple(pair):
        return pair[0], pair[1], pair[0] - pair[1]

    def spread(pair):
        return pair[0], pair[1] - pair[0], pair[0] + pair[1]

    def add(total, k, w):
        terms = (k[2] * w[0], k[0] * w[1], k[1] * w[2])
        return terms if total is None else tuple(a + b for a, b in zip(total, terms))

    def settle(total):
        return total[0] + total[2], total[0] + total[1]

    def store(table, n, re, im, total, fresh):
        total = settle(total)
        if not fresh:
            total = (total[0] + table[n, re, :], total[1] + table[n, im, :])
        table[n, re, :], table[n, im, :] = total

    def bins(p):
        return at(p * ROWS, ROWS), at(HALF + p * ROWS, ROWS)

    def sum_inputs(place, classes, fresh):
        base = place * PER_SPAN

        @pl.loop(0, HALF // ROWS)
        def _(p):
            re, im = bins(p)
            f = [triple((lag[m, re, :], lag[m, im, :])) for m in range(LAGS)]
            sums = [None] * PER_SPAN
            for i in range(PER_SPAN + LAGS - 1):
                if i % PER_SPAN in classes:
                    w = spread((win[base + i, re, :], win[base + i, im, :]))
                    for n in range(PER_SPAN):
                        if 0 <= i - n < LAGS:
                            sums[n] = add(sums[n], f[i - n], w)
            for n in range(PER_SPAN):
                store(acc, base + n, re, im, sums[n], fresh)

    def sum_early(chosen, fresh):
        spans = [i for i in range(WINDOWS) if i % PER_SPAN == chosen]

        @pl.loop(0, HALF // ROWS)
        def _(p):
            re, im = bins(p)
            f = [triple((lag[m, re, :], lag[m, im, :])) for m in range(LAGS)]
            sums = {}
            for i in spans:
                w = spread((win[i, re, :], win[i, im, :]))
                for n in range(max(0, i - LAGS + 1), min(BLOCKS - 1, i) + 1):
                    sums[n] = add(sums.get(n), f[i - n], w)
                    if i + PER_SPAN > n + LAGS - 1 or i + PER_SPAN >= WINDOWS:
                        store(acc, n, re, im, sums.pop(n), fresh)

    def sum_lags(classes, fresh):
        @pl.loop(0, HALF // ROWS)
        def _(p):
            re, im = bins(p)
            sums = [None] * LAGS
            for i in range(WINDOWS):
                if i % PER_SPAN in classes:
                    w = spread((win[i, re, :], win[i, im, :]))
                    for m in range(LAGS):
                        n = i - m
                        if 0 <= n < BLOCKS:
                            sums[m] = add(sums[m], triple((val[n, re, :], val[n, im, :])), w)
            for m in range(LAGS):
                store(acc_lag, m, re, im, sums[m], fresh)

    start(*direct(0))
    start(weight(0), weight(2))
    for k in range(1, GROUP):
        start(filter_to(k))
    start(*direct(1))
    for k in range(1, GROUP):
        start(values_to(k))
    weight(0).wait_recv()
    start(weight_along(1), weight_along(3), weight_over(0))
    pass_on(0)
    weight(2).wait_recv()
    start(weight_over(2))
    for k in (1, 3):
        weight_along(k).wait_recv()
        start(weight_over(k))
    filter_own.wait()
    for k in range(1, GROUP):
        filter_to(k).wait_recv()
    start(*[filter_along(k) for k in (2, 1, 3)])
    pass_on(1)
    for load in table_loads:
        load.wait()
    transform_values()
    own_load.wait()
    weight_load.wait()
    across(0)
    multiply(0, 0)
    for k in range(RING):
        weight_over(k).wait_recv()
    multiply(1, 0)
    pass_on(2)
    across(1)
    multiply(1, 1)
    multiply(0, 1)
    add_up(0)
    pass_on(3)
    across(2)
    multiply(1, 2)
    multiply(0, 2)
    pass_on(4)
    transform_filter()
    add_up(1)
    edge(0)
    transform_blocks(0)
    across(3)
    multiply(1, 3)
    multiply(0, 3)
    across(4)
    multiply(1, 4)
    multiply(0, 4)
    edge(1)
    transform_blocks(1)
    join(0)
    add_up(2)
    sum_early(0, True)
    sum_lags((0,), True)
    add_up(3)
    add_up(4)
    edge(2)
    transform_blocks(2)
    join(1)
    sum_early(1, False)
    sum_lags((1,), False)
    edge(3)
    edge(4)
    transform_blocks(PER_SPAN - 1)
    join(2)
    join(3)

    def finish_span(k):
        place = (q + k) % GROUP
        sum_inputs(place, (2, 3), False)
        for n in range(PER_SPAN // 2):
            base = place * PER_SPAN + 2 * n
            wide = backward(jnp.concatenate([acc[base], acc[base + 1]], axis=1))
            for e in range(2):
                out_buf[place, (2 * n + e) * BLOCK:(2 * n + e + 1) * BLOCK, :] = wide[:, e * LANES:(e + 1) * LANES]
        if k:
            start(out_to(k))

    settled = len(sends)
    finish_span(2)
    sum_lags((2, 3), False)
    for k in (2, 1, 3, 0):
        place = (z + k) % RING
        wide = backward(jnp.concatenate([acc_lag[2 * place], acc_lag[2 * place + 1]], axis=1))
        for e in range(2):
            lag_out[at((2 * place + e) * BLOCK, BLOCK), :] = wide[:, e * LANES:(e + 1) * LANES]
        if k:
            start(lag_along(k))
    finish_span(3)
    finish_span(1)
    finish_span(0)
    out_ref[:, at(q * LANES, LANES)] = out_buf[q]
    for copy in sends[:settled]:
        copy.wait_send()
    total = lag_out[at(z * LAG_SHARE, LAG_SHARE), :].astype(jnp.float32)
    for k in range(1, RING):
        lag_along(k).wait_recv()
        total = total + lag_got[(z + RING - k) % RING].astype(jnp.float32)
    lag_sum[...] = total * (1.0 / math.sqrt(SPAN * SPANS))
    for k in (2, 3, 1):
        start(lag_to(k))
    fg_ref[:, at(q * LANES, LANES)] = lag_sum[at(q * LAG_ROWS, LAG_ROWS), :]
    for copy in sends[settled:]:
        copy.wait_send()
    for k in range(1, GROUP):
        out_to(k).wait_recv()
        lag_to(k).wait_recv()


def hand_over(out_ref, fg_ref, out_final, fg_final, out_mid, fg_mid, sems):
    parts = [(out_ref, out_mid, out_final, pl.ds(n * BLOCK, BLOCK)) for n in range(PER_SPAN)]
    parts.append((fg_ref, fg_mid, fg_final, pl.ds(0, LAG_ROWS)))
    arrive = [
        pltpu.make_async_copy(a.at[rows], b.at[rows], sems.at[0, n])
        for n, (a, b, _, rows) in enumerate(parts)
    ]
    leave = [
        pltpu.make_async_copy(b.at[rows], c.at[rows], sems.at[1, n])
        for n, (_, b, c, rows) in enumerate(parts)
    ]
    for copy in arrive:
        copy.start()
    for first, second in zip(arrive, leave):
        first.wait()
        second.start()
    for copy in leave:
        copy.wait()


def per_device(inputs, out_grad, out_weight, filt):
    vmem = pl.BlockSpec(memory_space=pltpu.VMEM)
    anywhere = pl.BlockSpec(memory_space=pl.ANY)
    bf16, f32 = jnp.bfloat16, jnp.float32
    steps = len(STEPS)
    counts = [(4, steps)] * 2 + [(2 * RING,)] * 2 + [(2, GROUP)] * 2 + [(GROUP,)] * 2
    counts += [(2, GROUP, steps)] * 2 + [(2, steps)] * 2 + [(GROUP,)] * 2 + [(2, GROUP)] * 2 + [(8,)]
    results = pl.pallas_call(
        kernel,
        out_shape=(
            jax.ShapeDtypeStruct((SPAN, WIDTH), bf16),
            jax.ShapeDtypeStruct((LAG_ROWS, WIDTH), f32),
        ),
        in_specs=[anywhere] * 8,
        out_specs=(vmem, vmem),
        scratch_shapes=[
            pltpu.VMEM((SPAN, WIDTH), bf16),
            pltpu.VMEM((WIDTH, SHARE), bf16),
            pltpu.VMEM((FRAME, BLOCK), bf16),
            pltpu.VMEM((FRAME, BLOCK), bf16),
            pltpu.VMEM((BLOCK, FRAME), bf16),
            pltpu.VMEM((BLOCK, FRAME), bf16),
            pltpu.VMEM((WINDOWS + 1, FRAME, LANES), f32),
            pltpu.VMEM((3, SPAN, WIDTH), bf16),
            pltpu.VMEM((WIDTH, SHARE), bf16),
            pltpu.VMEM((LAG_LEN, LANES), f32),
            pltpu.VMEM((GROUP * SPAN, LANES), bf16),
            pltpu.VMEM((2, GROUP, SPAN, LANES), bf16),
            pltpu.VMEM((2, GROUP, SPAN, LANES), bf16),
            pltpu.VMEM(((GROUP + 2) * SPAN, LANES), bf16),
            pltpu.VMEM((WINDOWS, FRAME, LANES), f32),
            pltpu.VMEM((LAGS, FRAME, LANES), f32),
            pltpu.VMEM((BLOCKS, FRAME, LANES), f32),
            pltpu.VMEM((BLOCKS, FRAME, LANES), f32),
            pltpu.VMEM((LAGS, FRAME, LANES), f32),
            pltpu.VMEM((LAG_LEN, LANES), bf16),
            pltpu.VMEM((RING, LAG_SHARE, LANES), bf16),
            pltpu.VMEM((LAG_SHARE, LANES), f32),
            pltpu.VMEM((GROUP, SPAN, LANES), bf16),
        ] + [pltpu.SemaphoreType.DMA(count) for count in counts],
        compiler_params=pltpu.CompilerParams(
            collective_id=0, has_side_effects=True, vmem_limit_bytes=60 << 20
        ),
        cost_estimate=pl.CostEstimate(
            flops=20_000_000_000, bytes_accessed=12 << 20, transcendentals=0
        ),
        name="hyena_back",
    )(inputs, out_grad, out_weight, filt, *tables())
    return pl.pallas_call(
        hand_over,
        out_shape=tuple(jax.ShapeDtypeStruct(r.shape, r.dtype) for r in results),
        in_specs=[anywhere] * 2,
        out_specs=(anywhere, anywhere),
        scratch_shapes=[
            pltpu.VMEM((SPAN, WIDTH), bf16),
            pltpu.VMEM((LAG_ROWS, WIDTH), f32),
            pltpu.SemaphoreType.DMA((2, PER_SPAN + 1)),
        ],
        name="hand_over",
    )(*results)


def solution(mesh):
    in_specs = (P("seq", "chan"), P("seq", "chan"), P("chan", None), P("seq", "chan"))
    out_specs = (P("seq", "chan"), P("seq", "chan"))
    return jax.shard_map(
        per_device, mesh=mesh, in_specs=in_specs, out_specs=out_specs, check_vma=False
    )
```
